256 devices in a mesh: mem: 8 (over y, x_lo), space: 32 (over z, x_hi, core).
Axes of the slice: x: 4 (x_hi: 2, x_lo: 2; x = x_hi * 2 + x_lo), y: 4, z: 8, core: 2. Of those that a mesh axis runs over, the one named last changes fastest.
Arguments:
- state: float32 [32, 5, 256, 16, 256], P('mem', None, 'space'), may hold values from -6 to 6
- diffusion: float32 [5], replicated, may hold values from 0.1 to 0.5
- radius: int32 [16], replicated, may hold values from 4 to 8, as said below
- obs_cells: int32 [32, 128], P('space'), may hold values from 0 to 2047
- obs_count: int32 [32], P('space'), may hold values from 1 to 128, as said below
- obs_value: float32 [32, 128], P('space'), may hold values from -4 to 12
- obs_error: float32 [32, 128], P('space'), may hold values from 0.5 to 2
Outputs:
- analysis: float32 [32, 5, 256, 16, 256], P('mem', None, 'space')
The draws below stay inside these ranges and needn't reach their ends.
Inputs may be any that keep to these rules, and one draw needn't show every extreme that they name: Some level has radius exactly 8. Only the first obs_count[t] entries of a tile's lists are sites; some tile has exactly 128 sites.
All inputs are finite; a program needn't handle non-finite values.
Results may differ from the reference program's by a relative error of at most 0.0003.
Values sent between devices are 32-bit elements; how exact they have to be, the bound alone decides.
No kernel may reach another device: no remote copies, remote signals or barrier semaphores. Data moves between devices by JAX's collectives and lax.ppermute only.
A program may use at most 64 MiB of HBM per device.

```python
import math
import jax
import jax.numpy as jnp
from jax import lax

F = 5
CX = 8
NY = 256
NZ = 16
OBS_MAX = 128
MEMBERS = 32
TILES = 32
NX = 256


def draw_radius(key, part):
    key_one, key_two = jax.random.split(jax.random.fold_in(key, 11))
    levels = jax.random.randint(key_one, (NZ,), CX // 2, CX + 1, dtype=jnp.int32)
    chosen = jax.random.randint(key_two, (), 0, NZ, dtype=jnp.int32)
    return jnp.where(jnp.arange(NZ, dtype=jnp.int32) == chosen, CX, levels).astype(jnp.int32)


def draw_obs_count(key, part):
    key_one, key_two = jax.random.split(jax.random.fold_in(key, 23))
    counts = jax.random.randint(key_one, (TILES,), 1, OBS_MAX + 1, dtype=jnp.int32)
    chosen = jax.random.randint(key_two, (), 0, TILES, dtype=jnp.int32)
    return jnp.where(jnp.arange(TILES, dtype=jnp.int32) == chosen, OBS_MAX, counts).astype(jnp.int32)


def draw_obs_value(key, part):
    key_one = jax.random.fold_in(jax.random.fold_in(key, 37), 0)
    noise = jnp.clip(jax.random.normal(key_one, (TILES, OBS_MAX), jnp.float32), -4.0, 4.0)
    return noise.astype(jnp.float32)


def set_ends(drawn, rng, low, top_value):
    longest = drawn.shape.index(max(drawn.shape))
    spots = []
    for shift in (0, 1):
        where = [jax.random.randint(jax.random.fold_in(rng, axis), (), 0, length) for axis, length in enumerate(drawn.shape)]
        where[longest] = (where[longest] + shift) % drawn.shape[longest]
        spots.append(tuple(where))
    return drawn.at[spots[0]].set(low).at[spots[1]].set(top_value)


def steps_of(stream_key, extent, cuts, low, top_value):
    level = 1.0
    for axis_at, parts in cuts:
        steps = jax.random.uniform(jax.random.fold_in(jax.random.fold_in(stream_key, 6), axis_at), (parts,), jnp.float32, low / len(cuts), top_value / len(cuts))
        level = level * jnp.repeat(jnp.exp(steps), extent[axis_at] // parts).reshape((-1,) + (1,) * (len(extent) - 1 - axis_at))
    return level


def centred(key, shape, scale, bound, shards=(), kind=jnp.bfloat16):
    result = jax.random.normal(key, shape, jnp.float32) * scale
    if len(shards) > 0:
        result = steps_of(key, shape, shards, -0.22, 0.18) * result
    return jnp.clip(result, min=-bound, max=bound).astype(kind)


def setup_inputs(seed: int = 0) -> dict:
    keys = jax.random.split(jax.random.key(seed), 8)
    return {
        "state": centred(keys[0], (MEMBERS, F, NX, NZ, NY), 1.0, 6.0, ((0, 8), (2, 32)), jnp.float32),
        "diffusion": jnp.clip(jnp.exp(jax.random.uniform(keys[1], (F,), jnp.float32, math.log(0.1), math.log(0.5))), 0.1, 0.5),
        "radius": draw_radius(jax.random.fold_in(keys[7], 71), 0),
        "obs_cells": set_ends(jax.random.randint(keys[3], (TILES, OBS_MAX), 0, CX * NY), jax.random.fold_in(keys[3], 1), 0, (CX * NY) - 1).astype(jnp.int32),
        "obs_count": draw_obs_count(jax.random.fold_in(keys[7], 71), 0),
        "obs_value": draw_obs_value(jax.random.fold_in(keys[7], 71), 0),
        "obs_error": jnp.clip(jnp.exp(math.log(2.0) - 1.3862944 * jax.random.uniform(keys[6], (TILES, OBS_MAX), jnp.float32) ** steps_of(keys[6], (TILES, OBS_MAX), ((0, 32),), -0.2, 0.2)), 0.5, 2.0),
    }


time_step = 0.2
blend_share = 0.5


def advance(padded, diffuse_rate):
    interior = padded[..., 1:-1, :, :]
    east_side = padded[..., 2:, :, :]
    west_side = padded[..., :-2, :, :]
    north_side = jnp.roll(interior, -1, axis=-1)
    south_side = jnp.roll(interior, 1, axis=-1)
    wind_east = interior[..., 0:1, :, :, :]
    wind_north = interior[..., 1:2, :, :, :]
    transport = wind_east * (east_side - west_side) * 0.5 + wind_north * (north_side - south_side) * 0.5
    spread = east_side + west_side + north_side + south_side - 4.0 * interior
    return interior + time_step * (diffuse_rate * spread - transport)


def tile_weights(misfit3, x_sites, y_sites, inverse):
    cell_index = jnp.arange(CX * NY, dtype=jnp.int32)
    cell_east = cell_index // NY
    cell_north = cell_index % NY
    delta_east = cell_east[:, None] - x_sites[None, :]
    delta_north = (cell_north[:, None] - y_sites[None, :] + NY // 2) % NY - NY // 2
    distance_sq = (delta_east * delta_east + delta_north * delta_north).astype(jnp.float32)

    def level_weights(inverse_level):
        taper = jnp.maximum(0.0, 1.0 - distance_sq * inverse_level) ** 2
        return -0.5 * jnp.einsum("mo,co->mc", misfit3, taper, precision=lax.Precision.HIGHEST)

    return lax.map(level_weights, inverse)


def reference(state, diffusion, radius, obs_cells, obs_count, obs_value, obs_error):
    diffuse_rate = diffusion.reshape(F, 1, 1, 1)

    def evolve(member):
        for sweep_index in range(2):
            padded = jnp.concatenate([member[..., -1:, :, :], member, member[..., :1, :, :]], axis=-3)
            member = advance(padded, diffuse_rate)
        return member

    advected = lax.map(evolve, state)
    column = jnp.mean(advected[:, 2], axis=2)
    column_tiles = column.reshape(MEMBERS, TILES, CX * NY)
    observed = jnp.take_along_axis(column_tiles, obs_cells[None, :, :], axis=2)
    innovation = obs_value[None, :, :] - observed
    is_valid = (jnp.arange(OBS_MAX, dtype=jnp.int32)[None, :] < obs_count[:, None]).astype(jnp.float32)
    misfit = is_valid[None] * (innovation * innovation) / (obs_error * obs_error)[None]
    radius_float = radius.astype(jnp.float32)
    inverse = 1.0 / (radius_float * radius_float)
    offsets = jnp.arange(3, dtype=jnp.int32) - 1

    def one_tile(tile_index):
        neighbour = (tile_index + offsets) % TILES
        misfit3 = misfit[:, neighbour, :].reshape(MEMBERS, 3 * OBS_MAX)
        cells3 = obs_cells[neighbour]
        x_sites = (cells3 // NY + offsets[:, None] * CX).reshape(-1)
        y_sites = (cells3 % NY).reshape(-1)
        return tile_weights(misfit3, x_sites, y_sites, inverse)

    per_tile = lax.map(one_tile, jnp.arange(TILES, dtype=jnp.int32))
    per_tile = per_tile.reshape(TILES, NZ, MEMBERS, CX, NY)
    log_weight = per_tile.transpose(2, 0, 3, 1, 4).reshape(MEMBERS, NX, NZ, NY)
    best_log = jnp.max(log_weight, axis=0)
    expo_weight = jnp.exp(log_weight - best_log[None])
    weight_total = jnp.sum(expo_weight, axis=0)
    weighted = jnp.einsum("mxzy,mfxzy->fxzy", expo_weight, advected, precision=lax.Precision.HIGHEST)
    local_mean = weighted / weight_total[None]
    return advected + blend_share * (local_mean[None] - advected)
```

```python
import jax
import jax.numpy as jnp
import numpy as np
from jax import lax
from jax.experimental import pallas as pl
from jax.experimental.pallas import tpu as pltpu
from jax.sharding import PartitionSpec as P

time_step = 0.2
blend_share = 0.5
radii = (4, 5, 6, 7, 8)
reach = 7
f32 = jnp.float32
edge_rows = (0, 1, 6, 7)
smem = pl.BlockSpec(memory_space=pltpu.SMEM)
vmem = pl.BlockSpec(memory_space=pltpu.VMEM)


def taper_of(distance_sq, radius):
    inverse = np.float32(1.0) / np.float32(radius * radius)
    share = max(np.float32(0.0), np.float32(1.0) - np.float32(distance_sq) * inverse)
    return float(np.float32(share * share))


def step_row(centre, west, east, u_part, v_part, rate):
    size = centre.shape[-1]
    north = pltpu.roll(centre, size - 1, 1)
    south = pltpu.roll(centre, 1, 1)
    spread = (east + west) + (north + south) - 4.0 * centre
    return centre + (rate * spread - (u_part * (east - west) + v_part * (north - south)))


def interior_kernel(state, diffusion, cells, count, value, error, once, inner, column, grids):
    sites = cells.shape[1]
    lat_cells = state.shape[4]
    half = 0.5 * time_step

    def member(m, carry):
        for f in range(5):
            rate = diffusion[f] * time_step
            for x in range(1, 7):
                once[m, f, x - 1] = step_row(
                    state[m, f, x],
                    state[m, f, x - 1],
                    state[m, f, x + 1],
                    half * state[m, 0, x],
                    half * state[m, 1, x],
                    rate,
                )
        for f in range(5):
            rate = diffusion[f] * time_step
            for x in range(2, 6):
                row = step_row(
                    once[m, f, x - 1],
                    once[m, f, x - 2],
                    once[m, f, x],
                    half * once[m, 0, x - 1],
                    half * once[m, 1, x - 1],
                    rate,
                )
                inner[m, f, x - 2] = row
                if f == 2:
                    column[m, pl.ds(x - 2, 1)] = jnp.mean(row, axis=0, keepdims=True)
        return carry

    lax.fori_loop(0, state.shape[0], member, 0)

    cell = cells[...]
    site_x = cell // lat_cells
    site_y = cell % lat_cells
    valid = lax.broadcasted_iota(jnp.int32, (1, sites), 1) < count[0]
    weight = jnp.where(valid, 1.0 / (error[...] * error[...]), 0.0)
    moments = jnp.concatenate([weight, weight * value[...], weight * value[...] * value[...]], axis=0)
    at_x = lax.broadcasted_iota(jnp.int32, (8, sites), 0) == site_x
    at_y = (lax.broadcasted_iota(jnp.int32, (lat_cells, sites), 0) == site_y).astype(f32)
    stacked = jnp.concatenate(
        [jnp.where(at_x, moments[k : k + 1], 0.0) for k in range(3)], axis=0
    )
    sums = lax.dot_general(
        stacked, at_y, (((1,), (1,)), ((), ())), precision=lax.Precision.HIGHEST, preferred_element_type=f32
    )
    total, first, second = sums[0:8], sums[8:16], sums[16:24]
    mean = jnp.where(total > 0.0, first / jnp.where(total > 0.0, total, 1.0), 0.0)
    grids[0] = total
    grids[1] = mean
    grids[2] = second - first * mean


def first_rows(m, f, h, state, west, east, winds, rate):
    far_w, near_w = west[m, h, 0], west[m, h, 1]
    near_e, far_e = east[m, h, 0], east[m, h, 1]
    return (
        step_row(near_w, far_w, state[m, f, 0], *winds[0], rate),
        step_row(state[m, f, 0], near_w, state[m, f, 1], *winds[1], rate),
        step_row(state[m, f, 7], state[m, f, 6], near_e, *winds[2], rate),
        step_row(near_e, state[m, f, 7], far_e, *winds[3], rate),
    )


def second_rows(m, f, rows, once, winds, rate):
    return (
        step_row(rows[1], rows[0], once[m, f, 0], *winds[0], rate),
        step_row(once[m, f, 0], rows[1], once[m, f, 1], *winds[1], rate),
        step_row(once[m, f, 5], once[m, f, 4], rows[2], *winds[2], rate),
        step_row(rows[2], once[m, f, 5], rows[3], *winds[3], rate),
    )


def raw_winds(m, state, west, east):
    half = 0.5 * time_step
    return tuple(
        (half * pair[0], half * pair[1])
        for pair in (
            (west[m, 0, 1], west[m, 1, 1]),
            (state[m, 0, 0], state[m, 1, 0]),
            (state[m, 0, 7], state[m, 1, 7]),
            (east[m, 0, 0], east[m, 1, 0]),
        )
    )


def edge_kernel(state, diffusion, west, east, once, column, grids, edge, winds_out, grid):
    half = 0.5 * time_step

    def member(m, carry):
        winds = raw_winds(m, state, west, east)
        rows = [
            first_rows(m, f, f, state, west, east, winds, diffusion[f] * time_step) for f in range(3)
        ]
        after = []
        for k, (u_row, v_row) in enumerate(
            (
                (rows[0][1], rows[1][1]),
                (once[m, 0, 0], once[m, 1, 0]),
                (once[m, 0, 5], once[m, 1, 5]),
                (rows[0][2], rows[1][2]),
            )
        ):
            pair = (half * u_row, half * v_row)
            winds_out[m, 0, k] = pair[0]
            winds_out[m, 1, k] = pair[1]
            after.append(pair)
        means = []
        for f in (2, 0, 1):
            done = second_rows(m, f, rows[f], once, after, diffusion[f] * time_step)
            for k in range(4):
                edge[m, f, k] = done[k]
                if f == 2:
                    means.append(jnp.mean(done[k], axis=0, keepdims=True))
        inside = column[m]
        full = jnp.concatenate([means[0], means[1], inside, means[2], means[3]], axis=0)
        off = full - grids[1]
        grid[m] = grids[0] * (off * off) + grids[2]
        return carry

    lax.fori_loop(0, state.shape[0], member, 0)


def edge_rest_kernel(state, diffusion, west_winds, east_winds, west, east, once, winds_in, edge):
    def member(m, carry):
        winds = raw_winds(m, state, west_winds, east_winds)
        after = [(winds_in[m, 0, k], winds_in[m, 1, k]) for k in range(4)]
        for f in (3, 4):
            rate = diffusion[f] * time_step
            rows = first_rows(m, f, f - 3, state, west, east, winds, rate)
            done = second_rows(m, f, rows, once, after, rate)
            for k in range(4):
                edge[m, f - 3, k] = done[k]
        return carry

    lax.fori_loop(0, state.shape[0], member, 0)


def by_level(rows, level_radius):
    result = jnp.broadcast_to(rows[0], level_radius.shape)
    for k in range(1, len(radii)):
        result = jnp.where(level_radius == radii[k], rows[k], result)
    return result


def weights_kernel(level_radius, own, before, after, inner, edge, rest, sends, near, shifted, expo):
    members, width, lat_cells = own.shape

    def convolve(m, carry):
        near[0:8] = before[m]
        near[8:16] = own[m]
        near[16:24] = after[m]
        grid = near[...]
        shifted[0] = grid
        for dy in range(1, reach + 1):
            shifted[dy] = pltpu.roll(grid, dy, 1) + pltpu.roll(grid, lat_cells - dy, 1)
        sums = [None] * len(radii)
        for dx in range(reach + 1):
            for dy in range(reach + 1):
                distance_sq = dx * dx + dy * dy
                if distance_sq >= radii[-1] ** 2:
                    continue
                if dx == 0:
                    pair = shifted[dy, 8:16]
                else:
                    pair = shifted[dy, 8 + dx : 16 + dx] + shifted[dy, 8 - dx : 16 - dx]
                for k, radius in enumerate(radii):
                    if distance_sq < radius * radius:
                        term = pair * (-0.5 * taper_of(distance_sq, radius))
                        sums[k] = term if sums[k] is None else sums[k] + term
        for k in range(len(radii)):
            expo[m, k] = sums[k]
        return carry

    lax.fori_loop(0, members, convolve, 0)
    for k in range(len(radii)):
        logs = [expo[m, k] for m in range(members)]
        best = logs[0]
        for m in range(1, members):
            best = jnp.maximum(best, logs[m])
        total = None
        for m in range(members):
            value = jnp.exp(logs[m] - best)
            expo[m, k] = value
            total = value if total is None else total + value
        for x in range(width):
            sends[x, 80 + k : 81 + k] = best[x : x + 1]
            sends[x, 85 + k : 86 + k] = total[x : x + 1]
    for x in range(width):
        sends[x, 90:96] = jnp.zeros((6, lat_cells), f32)
        sums = [None] * 5
        for m in range(members):
            weight = by_level([expo[m, k, x : x + 1] for k in range(len(radii))], level_radius[...])
            for f in range(5):
                if x in edge_rows:
                    k = edge_rows.index(x)
                    row = edge[m, f, k] if f < 3 else rest[m, f - 3, k]
                else:
                    row = inner[m, f, x - 2]
                term = weight * row
                sums[f] = term if sums[f] is None else sums[f] + term
        for f in range(5):
            sends[x, 16 * f : 16 * f + 16] = sums[f]


def combine_kernel(level_radius, parts, result):
    sources = parts.shape[0]
    logs = [parts[d, 80:85] for d in range(sources)]
    best = logs[0]
    for d in range(1, sources):
        best = jnp.maximum(best, logs[d])
    scales = [jnp.exp(logs[d] - best) for d in range(sources)]
    total = None
    for d in range(sources):
        term = scales[d] * parts[d, 85:90]
        total = term if total is None else total + term
    over = 1.0 / total
    sums = [None] * 5
    for d in range(sources):
        share = scales[d] * over
        weight = by_level([share[k : k + 1] for k in range(len(radii))], level_radius[...])
        for f in range(5):
            term = weight * parts[d, 16 * f : 16 * f + 16]
            sums[f] = term if sums[f] is None else sums[f] + term
    for f in range(5):
        for d in range(sources):
            result[d, 16 * f : 16 * f + 16] = sums[f]


def blend_kernel(mean, inner, edge, rest, out):
    for f in range(5):
        for x in range(8):
            if x in edge_rows:
                k = edge_rows.index(x)
                row = edge[0, f, k] if f < 3 else rest[0, f - 3, k]
            else:
                row = inner[0, f, x - 2]
            out[0, f, x] = row + blend_share * (mean[x, 16 * f : 16 * f + 16] - row)


def local(state, diffusion, radius, obs_cells, obs_count, obs_value, obs_error):
    members, fields, width, levels, lat_cells = state.shape
    size = lax.axis_size("space")
    up = [(i, (i + 1) % size) for i in range(size)]
    down = [(j, i) for i, j in up]

    def shape(*dims):
        return jax.ShapeDtypeStruct(dims, f32)

    west_a = lax.ppermute(state[:, :3, 6:8], "space", up)
    east_a = lax.ppermute(state[:, :3, 0:2], "space", down)
    west_b = lax.ppermute(state[:, 3:, 6:8], "space", up)
    east_b = lax.ppermute(state[:, 3:, 0:2], "space", down)
    level_radius = jnp.broadcast_to(radius[:, None], (levels, lat_cells))

    once, inner, column, grids = pl.pallas_call(
        interior_kernel,
        out_shape=(
            shape(members, fields, 6, levels, lat_cells),
            shape(members, fields, 4, levels, lat_cells),
            shape(members, 4, lat_cells),
            shape(3, width, lat_cells),
        ),
        in_specs=[vmem, smem, vmem, smem, vmem, vmem],
        name="interior",
    )(state, diffusion, obs_cells, obs_count, obs_value, obs_error)
    edge, winds, grid = pl.pallas_call(
        edge_kernel,
        out_shape=(
            shape(members, 3, 4, levels, lat_cells),
            shape(members, 2, 4, levels, lat_cells),
            shape(members, width, lat_cells),
        ),
        in_specs=[vmem, smem] + [vmem] * 5,
        name="edges",
    )(state, diffusion, west_a, east_a, once, column, grids)
    before = lax.ppermute(grid, "space", up)
    after = lax.ppermute(grid, "space", down)
    rest = pl.pallas_call(
        edge_rest_kernel,
        out_shape=shape(members, 2, 4, levels, lat_cells),
        in_specs=[vmem, smem] + [vmem] * 6,
        name="edges_rest",
    )(state, diffusion, west_a, east_a, west_b, east_b, once, winds)
    sends = pl.pallas_call(
        weights_kernel,
        out_shape=shape(width, 96, lat_cells),
        in_specs=[vmem] * 7,
        scratch_shapes=[
            pltpu.VMEM((24, lat_cells), f32),
            pltpu.VMEM((8, 24, lat_cells), f32),
            pltpu.VMEM((members, len(radii), width, lat_cells), f32),
        ],
        name="weights",
    )(level_radius, grid, before, after, inner, edge, rest)
    parts = lax.all_to_all(sends, "mem", 0, 0, tiled=True)
    share = pl.pallas_call(
        combine_kernel, out_shape=shape(width, 80, lat_cells), in_specs=[vmem] * 2, name="combine"
    )(level_radius, parts)
    mean = lax.all_to_all(share, "mem", 0, 0, tiled=True)

    def per_member(*dims):
        return pl.BlockSpec((1,) + dims, lambda m: (m, 0, 0, 0, 0))

    return pl.pallas_call(
        blend_kernel,
        grid=(members,),
        out_shape=shape(*state.shape),
        in_specs=[
            pl.BlockSpec((width, 80, lat_cells), lambda m: (0, 0, 0)),
            per_member(fields, 4, levels, lat_cells),
            per_member(3, 4, levels, lat_cells),
            per_member(2, 4, levels, lat_cells),
        ],
        out_specs=per_member(fields, width, levels, lat_cells),
        name="blend",
    )(mean, inner, edge, rest)


def solution(mesh):
    return jax.shard_map(
        local,
        mesh=mesh,
        in_specs=(
            P("mem", None, "space", None, None),
            P(),
            P(),
            P("space", None),
            P("space"),
            P("space", None),
            P("space", None),
        ),
        out_specs=P("mem", None, "space", None, None),
        check_vma=False,
    )
```

```python
import jax
import jax.numpy as jnp
import numpy as np
from jax import lax
from jax.experimental import pallas as pl
from jax.experimental.pallas import tpu as pltpu
from jax.sharding import PartitionSpec as P

time_step = 0.2
blend_share = 0.5
radii = (4, 5, 6, 7, 8)
reach = 7
f32 = jnp.float32
edge_rows = (0, 1, 6, 7)
smem = pl.BlockSpec(memory_space=pltpu.SMEM)
vmem = pl.BlockSpec(memory_space=pltpu.VMEM)
room = pltpu.CompilerParams(vmem_limit_bytes=16 << 20)


def taper_of(distance_sq, radius):
    inverse = np.float32(1.0) / np.float32(radius * radius)
    share = max(np.float32(0.0), np.float32(1.0) - np.float32(distance_sq) * inverse)
    return float(np.float32(share * share))


def step_row(centre, west, east, u_part, v_part, rate):
    size = centre.shape[-1]
    north = pltpu.roll(centre, size - 1, 1)
    south = pltpu.roll(centre, 1, 1)
    spread = (east + west) + (north + south) - 4.0 * centre
    return centre + (rate * spread - (u_part * (east - west) + v_part * (north - south)))


def interior_kernel(state, diffusion, cells, count, value, error, once, inner, column, grids):
    sites = cells.shape[1]
    lat_cells = state.shape[4]
    half = 0.5 * time_step

    def member(m, carry):
        for f in range(5):
            rate = diffusion[f] * time_step
            for x in range(1, 7):
                once[m, f, x - 1] = step_row(
                    state[m, f, x],
                    state[m, f, x - 1],
                    state[m, f, x + 1],
                    half * state[m, 0, x],
                    half * state[m, 1, x],
                    rate,
                )
        for f in range(5):
            rate = diffusion[f] * time_step
            for x in range(2, 6):
                row = step_row(
                    once[m, f, x - 1],
                    once[m, f, x - 2],
                    once[m, f, x],
                    half * once[m, 0, x - 1],
                    half * once[m, 1, x - 1],
                    rate,
                )
                inner[m, f, x - 2] = row
                if f == 2:
                    column[m, pl.ds(x - 2, 1)] = jnp.mean(row, axis=0, keepdims=True)
        return carry

    lax.fori_loop(0, state.shape[0], member, 0)

    cell = cells[...]
    site_x = cell // lat_cells
    site_y = cell % lat_cells
    valid = lax.broadcasted_iota(jnp.int32, (1, sites), 1) < count[0]
    weight = jnp.where(valid, 1.0 / (error[...] * error[...]), 0.0)
    moments = jnp.concatenate([weight, weight * value[...], weight * value[...] * value[...]], axis=0)
    at_x = lax.broadcasted_iota(jnp.int32, (8, sites), 0) == site_x
    at_y = (lax.broadcasted_iota(jnp.int32, (lat_cells, sites), 0) == site_y).astype(f32)
    stacked = jnp.concatenate(
        [jnp.where(at_x, moments[k : k + 1], 0.0) for k in range(3)], axis=0
    )
    sums = lax.dot_general(
        stacked, at_y, (((1,), (1,)), ((), ())), precision=lax.Precision.HIGHEST, preferred_element_type=f32
    )
    total, first, second = sums[0:8], sums[8:16], sums[16:24]
    mean = jnp.where(total > 0.0, first / jnp.where(total > 0.0, total, 1.0), 0.0)
    grids[0] = total
    grids[1] = mean
    grids[2] = second - first * mean


def first_rows(m, f, h, state, west, east, winds, rate):
    far_w, near_w = west[m, h, 0], west[m, h, 1]
    near_e, far_e = east[m, h, 0], east[m, h, 1]
    return (
        step_row(near_w, far_w, state[m, f, 0], *winds[0], rate),
        step_row(state[m, f, 0], near_w, state[m, f, 1], *winds[1], rate),
        step_row(state[m, f, 7], state[m, f, 6], near_e, *winds[2], rate),
        step_row(near_e, state[m, f, 7], far_e, *winds[3], rate),
    )


def second_rows(m, f, rows, once, winds, rate):
    return (
        step_row(rows[1], rows[0], once[m, f, 0], *winds[0], rate),
        step_row(once[m, f, 0], rows[1], once[m, f, 1], *winds[1], rate),
        step_row(once[m, f, 5], once[m, f, 4], rows[2], *winds[2], rate),
        step_row(rows[2], once[m, f, 5], rows[3], *winds[3], rate),
    )


def raw_winds(m, state, west, east):
    half = 0.5 * time_step
    return tuple(
        (half * pair[0], half * pair[1])
        for pair in (
            (west[m, 0, 1], west[m, 1, 1]),
            (state[m, 0, 0], state[m, 1, 0]),
            (state[m, 0, 7], state[m, 1, 7]),
            (east[m, 0, 0], east[m, 1, 0]),
        )
    )


def edge_kernel(state, diffusion, west, east, once, column, grids, edge, winds_out, grid):
    half = 0.5 * time_step

    def member(m, carry):
        winds = raw_winds(m, state, west, east)
        rows = [
            first_rows(m, f, f, state, west, east, winds, diffusion[f] * time_step) for f in range(3)
        ]
        after = []
        for k, (u_row, v_row) in enumerate(
            (
                (rows[0][1], rows[1][1]),
                (once[m, 0, 0], once[m, 1, 0]),
                (once[m, 0, 5], once[m, 1, 5]),
                (rows[0][2], rows[1][2]),
            )
        ):
            pair = (half * u_row, half * v_row)
            winds_out[m, 0, k] = pair[0]
            winds_out[m, 1, k] = pair[1]
            after.append(pair)
        means = []
        for f in (2, 0, 1):
            done = second_rows(m, f, rows[f], once, after, diffusion[f] * time_step)
            for k in range(4):
                edge[m, f, k] = done[k]
                if f == 2:
                    means.append(jnp.mean(done[k], axis=0, keepdims=True))
        inside = column[m]
        full = jnp.concatenate([means[0], means[1], inside, means[2], means[3]], axis=0)
        off = full - grids[1]
        grid[m] = grids[0] * (off * off) + grids[2]
        return carry

    lax.fori_loop(0, state.shape[0], member, 0)


def edge_rest_kernel(state, diffusion, west_winds, east_winds, west, east, once, winds_in, edge):
    def member(m, carry):
        winds = raw_winds(m, state, west_winds, east_winds)
        after = [(winds_in[m, 0, k], winds_in[m, 1, k]) for k in range(4)]
        for f in (3, 4):
            rate = diffusion[f] * time_step
            rows = first_rows(m, f, f - 3, state, west, east, winds, rate)
            done = second_rows(m, f, rows, once, after, rate)
            for k in range(4):
                edge[m, f - 3, k] = done[k]
        return carry

    lax.fori_loop(0, state.shape[0], member, 0)


def by_level(rows, level_radius):
    result = jnp.broadcast_to(rows[0], level_radius.shape)
    for k in range(1, len(radii)):
        result = jnp.where(level_radius == radii[k], rows[k], result)
    return result


def weights_kernel(level_radius, own, before, after, inner, edge, rest, sends, near, shifted, expo):
    members, width, lat_cells = own.shape

    def convolve(m, carry):
        near[0:8] = before[m]
        near[8:16] = own[m]
        near[16:24] = after[m]
        grid = near[...]
        shifted[0] = grid
        for dy in range(1, reach + 1):
            shifted[dy] = pltpu.roll(grid, dy, 1) + pltpu.roll(grid, lat_cells - dy, 1)
        sums = [None] * len(radii)
        for dx in range(reach + 1):
            for dy in range(reach + 1):
                distance_sq = dx * dx + dy * dy
                if distance_sq >= radii[-1] ** 2:
                    continue
                if dx == 0:
                    pair = shifted[dy, 8:16]
                else:
                    pair = shifted[dy, 8 + dx : 16 + dx] + shifted[dy, 8 - dx : 16 - dx]
                for k, radius in enumerate(radii):
                    if distance_sq < radius * radius:
                        term = pair * (-0.5 * taper_of(distance_sq, radius))
                        sums[k] = term if sums[k] is None else sums[k] + term
        for k in range(len(radii)):
            expo[m, k] = sums[k]
        return carry

    lax.fori_loop(0, members, convolve, 0)
    for k in range(len(radii)):
        logs = [expo[m, k] for m in range(members)]
        best = logs[0]
        for m in range(1, members):
            best = jnp.maximum(best, logs[m])
        total = None
        for m in range(members):
            value = jnp.exp(logs[m] - best)
            expo[m, k] = value
            total = value if total is None else total + value
        for x in range(width):
            sends[x, 80 + k : 81 + k] = best[x : x + 1]
            sends[x, 85 + k : 86 + k] = total[x : x + 1]
    for x in range(width):
        sends[x, 90:96] = jnp.zeros((6, lat_cells), f32)
        sums = [None] * 5
        for m in range(members):
            weight = by_level([expo[m, k, x : x + 1] for k in range(len(radii))], level_radius[...])
            for f in range(5):
                if x in edge_rows:
                    k = edge_rows.index(x)
                    row = edge[m, f, k] if f < 3 else rest[m, f - 3, k]
                else:
                    row = inner[m, f, x - 2]
                term = weight * row
                sums[f] = term if sums[f] is None else sums[f] + term
        for f in range(5):
            sends[x, 16 * f : 16 * f + 16] = sums[f]


def combine_kernel(level_radius, parts, result):
    sources = parts.shape[0]
    logs = [parts[d, 80:85] for d in range(sources)]
    best = logs[0]
    for d in range(1, sources):
        best = jnp.maximum(best, logs[d])
    scales = [jnp.exp(logs[d] - best) for d in range(sources)]
    total = None
    for d in range(sources):
        term = scales[d] * parts[d, 85:90]
        total = term if total is None else total + term
    over = 1.0 / total
    sums = [None] * 5
    for d in range(sources):
        share = scales[d] * over
        weight = by_level([share[k : k + 1] for k in range(len(radii))], level_radius[...])
        for f in range(5):
            term = weight * parts[d, 16 * f : 16 * f + 16]
            sums[f] = term if sums[f] is None else sums[f] + term
    for f in range(5):
        for d in range(sources):
            result[d, 16 * f : 16 * f + 16] = sums[f]


def blend_kernel(mean, inner, edge, rest, out):
    for f in range(5):
        for x in range(8):
            if x in edge_rows:
                k = edge_rows.index(x)
                row = edge[0, f, k] if f < 3 else rest[0, f - 3, k]
            else:
                row = inner[0, f, x - 2]
            out[0, f, x] = row + blend_share * (mean[x, 16 * f : 16 * f + 16] - row)


def local(state, diffusion, radius, obs_cells, obs_count, obs_value, obs_error):
    members, fields, width, levels, lat_cells = state.shape
    size = lax.axis_size("space")
    up = [(i, (i + 1) % size) for i in range(size)]
    down = [(j, i) for i, j in up]

    def shape(*dims):
        return jax.ShapeDtypeStruct(dims, f32)

    west_a = lax.ppermute(state[:, :3, 6:8], "space", up)
    east_a = lax.ppermute(state[:, :3, 0:2], "space", down)
    west_b = lax.ppermute(state[:, 3:, 6:8], "space", up)
    east_b = lax.ppermute(state[:, 3:, 0:2], "space", down)
    level_radius = jnp.broadcast_to(radius[:, None], (levels, lat_cells))

    once, inner, column, grids = pl.pallas_call(
        interior_kernel,
        out_shape=(
            shape(members, fields, 6, levels, lat_cells),
            shape(members, fields, 4, levels, lat_cells),
            shape(members, 4, lat_cells),
            shape(3, width, lat_cells),
        ),
        in_specs=[vmem, smem, vmem, smem, vmem, vmem],
        name="interior",
        compiler_params=room,
    )(state, diffusion, obs_cells, obs_count, obs_value, obs_error)
    edge, winds, grid = pl.pallas_call(
        edge_kernel,
        out_shape=(
            shape(members, 3, 4, levels, lat_cells),
            shape(members, 2, 4, levels, lat_cells),
            shape(members, width, lat_cells),
        ),
        in_specs=[vmem, smem] + [vmem] * 5,
        name="edges",
        compiler_params=room,
    )(state, diffusion, west_a, east_a, once, column, grids)
    before = lax.ppermute(grid, "space", up)
    after = lax.ppermute(grid, "space", down)
    rest = pl.pallas_call(
        edge_rest_kernel,
        out_shape=shape(members, 2, 4, levels, lat_cells),
        in_specs=[vmem, smem] + [vmem] * 6,
        name="edges_rest",
        compiler_params=room,
    )(state, diffusion, west_a, east_a, west_b, east_b, once, winds)
    sends = pl.pallas_call(
        weights_kernel,
        out_shape=shape(width, 96, lat_cells),
        in_specs=[vmem] * 7,
        scratch_shapes=[
            pltpu.VMEM((24, lat_cells), f32),
            pltpu.VMEM((8, 24, lat_cells), f32),
            pltpu.VMEM((members, len(radii), width, lat_cells), f32),
        ],
        name="weights",
        compiler_params=room,
    )(level_radius, grid, before, after, inner, edge, rest)
    parts = lax.all_to_all(sends, "mem", 0, 0, tiled=True)
    share = pl.pallas_call(
        combine_kernel, out_shape=shape(width, 80, lat_cells), in_specs=[vmem] * 2, name="combine", compiler_params=room
    )(level_radius, parts)
    mean = lax.all_to_all(share, "mem", 0, 0, tiled=True)

    def per_member(*dims):
        return pl.BlockSpec((1,) + dims, lambda m: (m, 0, 0, 0, 0))

    return pl.pallas_call(
        blend_kernel,
        grid=(members,),
        out_shape=shape(*state.shape),
        in_specs=[
            pl.BlockSpec((width, 80, lat_cells), lambda m: (0, 0, 0)),
            per_member(fields, 4, levels, lat_cells),
            per_member(3, 4, levels, lat_cells),
            per_member(2, 4, levels, lat_cells),
        ],
        out_specs=per_member(fields, width, levels, lat_cells),
        name="blend",
        compiler_params=room,
    )(mean, inner, edge, rest)


def solution(mesh):
    return jax.shard_map(
        local,
        mesh=mesh,
        in_specs=(
            P("mem", None, "space", None, None),
            P(),
            P(),
            P("space", None),
            P("space"),
            P("space", None),
            P("space", None),
        ),
        out_specs=P("mem", None, "space", None, None),
        check_vma=False,
    )
```

```python
import jax
import jax.numpy as jnp
import numpy as np
from jax import lax
from jax.experimental import pallas as pl
from jax.experimental.pallas import tpu as pltpu
from jax.sharding import PartitionSpec as P

time_step = 0.2
blend_share = 0.5
radii = (4, 5, 6, 7, 8)
reach = 7
f32 = jnp.float32
anywhere = pl.BlockSpec(memory_space=pl.ANY)
smem = pl.BlockSpec(memory_space=pltpu.SMEM)
vmem = pl.BlockSpec(memory_space=pltpu.VMEM)
room = pltpu.CompilerParams(vmem_limit_bytes=16 << 20)


def taper_of(distance_sq, radius):
    inverse = np.float32(1.0) / np.float32(radius * radius)
    share = max(np.float32(0.0), np.float32(1.0) - np.float32(distance_sq) * inverse)
    return float(np.float32(share * share))


def step_row(centre, west, east, u_part, v_part, rate):
    size = centre.shape[-1]
    north = pltpu.roll(centre, size - 1, 1)
    south = pltpu.roll(centre, 1, 1)
    spread = (east + west) + (north + south) - 4.0 * centre
    return centre + (rate * spread - (u_part * (east - west) + v_part * (north - south)))


def natural(row, parity):
    return row + parity * (7 - 2 * row)


def step_inner(centre, inner, u_part, v_part, rate):
    size = centre.shape[-1]
    north = pltpu.roll(centre, size - 1, 1)
    south = pltpu.roll(centre, 1, 1)
    spread = inner + (north + south) - 4.0 * centre
    return centre + (rate * spread - (u_part * inner + v_part * (north - south)))


def interior_kernel(
    parity_ref, state, near, diffusion, radius, cells, count, value, error,
    core, once_one, pre_zero, pre_one, column, grids, level_radius, far, once,
):
    sites = cells.shape[1]
    lat_cells = state.shape[4]
    parity = parity_ref[0]
    half = 0.5 * time_step
    signed = half * (1 - 2 * parity).astype(f32)
    far_start = 6 * parity

    def member(m, carry):
        def at(f, k):
            if k < 8:
                return state[m, f, natural(k, parity)]
            return near[m, f, parity if k == 8 else 1 - parity]

        for k in range(1, 9):
            u_part, v_part = signed * at(0, k), half * at(1, k)
            for f in range(5):
                once[f, k - 1] = step_row(
                    at(f, k), at(f, k - 1), at(f, k + 1), u_part, v_part, diffusion[f] * time_step
                )
        u_part, v_part = signed * at(0, 0), half * at(1, 0)
        for f in range(5):
            pre_zero[m, f] = step_inner(at(f, 0), at(f, 1), u_part, v_part, diffusion[f] * time_step)
        u_part, v_part = signed * once[0, 0], half * once[1, 0]
        for f in range(5):
            pre_one[m, f] = step_inner(once[f, 0], once[f, 1], u_part, v_part, diffusion[f] * time_step)
            once_one[m, f] = once[f, 0]
        column[m] = jnp.zeros((8, lat_cells), f32)
        for k in range(2, 8):
            u_part, v_part = signed * once[0, k - 1], half * once[1, k - 1]
            for f in range(5):
                row = step_row(
                    once[f, k - 1], once[f, k - 2], once[f, k], u_part, v_part, diffusion[f] * time_step
                )
                core[m, f, k - 2] = row
                if f == 2:
                    column[m, pl.ds(natural(k, parity), 1)] = jnp.mean(row, axis=0, keepdims=True)
        for f in (3, 4):
            for k in range(2):
                far[m, f - 3, k] = state[m, f, far_start + k]
        return carry

    lax.fori_loop(0, state.shape[0], member, 0)

    cell = cells[...]
    site_x = cell // lat_cells
    site_y = cell % lat_cells
    valid = lax.broadcasted_iota(jnp.int32, (1, sites), 1) < count[0]
    weight = jnp.where(valid, 1.0 / (error[...] * error[...]), 0.0)
    moments = jnp.concatenate([weight, weight * value[...], weight * value[...] * value[...]], axis=0)
    at_x = lax.broadcasted_iota(jnp.int32, (8, sites), 0) == site_x
    at_y = (lax.broadcasted_iota(jnp.int32, (lat_cells, sites), 0) == site_y).astype(f32)
    stacked = jnp.concatenate(
        [jnp.where(at_x, moments[k : k + 1], 0.0) for k in range(3)], axis=0
    )
    sums = lax.dot_general(
        stacked, at_y, (((1,), (1,)), ((), ())), precision=lax.Precision.HIGHEST, preferred_element_type=f32
    )
    total, first, second = sums[0:8], sums[8:16], sums[16:24]
    mean = jnp.where(total > 0.0, first / jnp.where(total > 0.0, total, 1.0), 0.0)
    grids[0] = total
    grids[1] = mean
    grids[2] = second - first * mean
    levels = level_radius.shape[0]
    level = lax.broadcasted_iota(jnp.int32, (levels, lat_cells), 0)
    chosen = jnp.full((levels, lat_cells), radius[0], jnp.int32)
    for z in range(1, levels):
        chosen = jnp.where(level == z, radius[z], chosen)
    level_radius[...] = chosen


def far_rows(beyond, next_to, zero, once_one, pre_zero, pre_one, winds, rate):
    (u_beyond, v_beyond), (u_zero, _), (u_one, _) = winds
    outside = step_row(next_to, beyond, zero, u_beyond, v_beyond, rate)
    first = pre_zero + next_to * (rate + u_zero)

    def again(u_part, v_part):
        return (
            step_row(first, outside, once_one, u_part, v_part, rate),
            pre_one + first * (rate + u_one),
        )

    return first, again


def far_winds(m, parity, state, far, once_one):
    half = 0.5 * time_step
    signed = half * (1 - 2 * parity).astype(f32)
    row = natural(0, parity)
    return (
        (signed * far[m, 0, 1 - parity], half * far[m, 1, 1 - parity]),
        (signed * state[m, 0, row], None),
        (signed * once_one[m, 0], None),
    )


def far_kernel(
    parity_ref, state, diffusion, far, once_one, pre_zero, pre_one, column, grids, edge, winds_out, grid, full
):
    parity = parity_ref[0]
    half = 0.5 * time_step
    signed = half * (1 - 2 * parity).astype(f32)

    def member(m, carry):
        winds = far_winds(m, parity, state, far, once_one)
        pairs = [
            far_rows(
                far[m, f, parity], far[m, f, 1 - parity], state[m, f, natural(0, parity)],
                once_one[m, f], pre_zero[m, f], pre_one[m, f], winds, diffusion[f] * time_step,
            )
            for f in range(3)
        ]
        u_part, v_part = signed * pairs[0][0], half * pairs[1][0]
        winds_out[m, 0] = u_part
        winds_out[m, 1] = v_part
        full[m] = column[m]
        for f in (2, 0, 1):
            for k, row in enumerate(pairs[f][1](u_part, v_part)):
                edge[m, f, k] = row
                if f == 2:
                    full[m, pl.ds(natural(k, parity), 1)] = jnp.mean(row, axis=0, keepdims=True)
        off = full[m] - grids[1]
        grid[m] = grids[0] * (off * off) + grids[2]
        return carry

    lax.fori_loop(0, state.shape[0], member, 0, unroll=True)


def far_rest_kernel(parity_ref, state, diffusion, far_winds_ref, far, once_one, pre_zero, pre_one, winds_in, edge):
    parity = parity_ref[0]

    def member(m, carry):
        winds = far_winds(m, parity, state, far_winds_ref, once_one)
        for f in (3, 4):
            _, again = far_rows(
                far[m, f - 3, parity], far[m, f - 3, 1 - parity], state[m, f, natural(0, parity)],
                once_one[m, f], pre_zero[m, f], pre_one[m, f], winds, diffusion[f] * time_step,
            )
            for k, row in enumerate(again(winds_in[m, 0], winds_in[m, 1])):
                edge[m, f - 3, k] = row
        return carry

    lax.fori_loop(0, state.shape[0], member, 0, unroll=True)


def by_level(rows, level_radius):
    result = jnp.broadcast_to(rows[0], level_radius.shape)
    for k in range(1, len(radii)):
        result = jnp.where(level_radius == radii[k], rows[k], result)
    return result


def final_row(m, f, k, core, edge, rest):
    if k >= 2:
        return core[m, f, k - 2]
    return edge[m, f, k] if f < 3 else rest[m, f - 3, k]


def weights_kernel(parity_ref, level_radius, own, beside, beyond, core, edge, rest, sends, near, shifted, expo):
    members, width, lat_cells = own.shape
    half = lat_cells // 2
    parity = parity_ref[0]

    def convolve(m, carry):
        near[m, pl.ds(16 * parity, 8)] = beyond[m]
        near[m, 8:16] = own[m]
        near[m, pl.ds(16 * (1 - parity), 8)] = beside[m]
        grid = near[m]
        for h in range(2):
            shifted[m, 0, h] = grid[:, half * h : half * h + half]
        for dy in range(1, reach + 1):
            both = pltpu.roll(grid, dy, 1) + pltpu.roll(grid, lat_cells - dy, 1)
            for h in range(2):
                shifted[m, dy, h] = both[:, half * h : half * h + half]
        for h in range(2):
            sums = [None] * len(radii)
            for dx in range(reach + 1):
                for dy in range(reach + 1):
                    distance_sq = dx * dx + dy * dy
                    if distance_sq >= radii[-1] ** 2:
                        continue
                    if dx == 0:
                        pair = shifted[m, dy, h, 8:16]
                    else:
                        pair = shifted[m, dy, h, 8 + dx : 16 + dx] + shifted[m, dy, h, 8 - dx : 16 - dx]
                    for k, radius in enumerate(radii):
                        if distance_sq < radius * radius:
                            term = pair * (-0.5 * taper_of(distance_sq, radius))
                            sums[k] = term if sums[k] is None else sums[k] + term
            for k in range(len(radii)):
                expo[m, k, :, half * h : half * h + half] = sums[k]
        return carry

    lax.fori_loop(0, members, convolve, 0, unroll=True)
    for k in range(len(radii)):
        logs = [expo[m, k] for m in range(members)]
        best = logs[0]
        for m in range(1, members):
            best = jnp.maximum(best, logs[m])
        values = [jnp.exp(logs[m] - best) for m in range(members)]
        total = values[0]
        for m in range(1, members):
            total = total + values[m]
        over = 1.0 / total
        for m in range(members):
            expo[m, k] = values[m] * over
        level_log = best + jnp.log(total)
        for x in range(width):
            sends[natural(x, parity), 80 + k : 81 + k] = level_log[x : x + 1]
    for x in range(width):
        here = pl.ds(natural(x, parity), 1)
        sends[x, 85:88] = jnp.zeros((3, lat_cells), f32)
        sums = [None] * 5
        for m in range(members):
            weight = by_level([expo[m, k, here] for k in range(len(radii))], level_radius[...])
            for f in range(5):
                row = final_row(m, f, x, core, edge, rest)
                term = weight * row
                sums[f] = term if sums[f] is None else sums[f] + term
        for f in range(5):
            sends[x, 16 * f : 16 * f + 16] = sums[f]


def combine_kernel(level_radius, parts, result):
    sources = parts.shape[0]
    logs = [parts[d, 80:85] for d in range(sources)]
    best = logs[0]
    for d in range(1, sources):
        best = jnp.maximum(best, logs[d])
    scales = [jnp.exp(logs[d] - best) for d in range(sources)]
    total = scales[0]
    for d in range(1, sources):
        total = total + scales[d]
    over = 1.0 / total
    sums = [None] * 5
    for d in range(sources):
        share = scales[d] * over
        weight = by_level([share[k : k + 1] for k in range(len(radii))], level_radius[...])
        for f in range(5):
            term = weight * parts[d, 16 * f : 16 * f + 16]
            sums[f] = term if sums[f] is None else sums[f] + term
    for f in range(5):
        for d in range(sources):
            result[d, 16 * f : 16 * f + 16] = sums[f]


def blend_kernel(parity_ref, mean, core, edge, rest, out, done, sems):
    members = core.shape[0]
    parity = parity_ref[0]
    copies = []
    for m in range(members):
        for part in range(2):
            for k in range(4 * part, 4 * part + 4):
                for f in range(5):
                    row = final_row(m, f, k, core, edge, rest)
                    done[m, f, natural(k, parity)] = row + blend_share * (mean[k, 16 * f : 16 * f + 16] - row)
            rows = pl.ds(4 * (part + parity * (1 - 2 * part)), 4)
            copy = pltpu.make_async_copy(done.at[m, :, rows], out.at[m, :, rows], sems.at[m, part])
            copy.start()
            copies.append(copy)
    for copy in copies:
        copy.wait()


def local(state, diffusion, radius, obs_cells, obs_count, obs_value, obs_error):
    members, fields, width, levels, lat_cells = state.shape
    size = lax.axis_size("space")
    parity = (lax.axis_index("space") & 1).astype(jnp.int32).reshape(1)
    beside_pairs = [(i, i + 1 - 2 * (i % 2)) for i in range(size)]
    beyond_pairs = [(i, (i - 1 + 2 * (i % 2)) % size) for i in range(size)]

    def shape(*dims):
        return jax.ShapeDtypeStruct(dims, f32)

    near = lax.dynamic_slice_in_dim(state, 6 * (1 - parity[0]), 2, axis=2)
    far_a = lax.dynamic_slice_in_dim(state[:, :3], 6 * parity[0], 2, axis=2)
    near = lax.ppermute(near, "space", beside_pairs)
    far_a = lax.ppermute(far_a, "space", beyond_pairs)
    core, once_one, pre_zero, pre_one, column, grids, level_radius, far_b = pl.pallas_call(
        interior_kernel,
        out_shape=(
            shape(members, fields, 6, levels, lat_cells),
            shape(members, fields, levels, lat_cells),
            shape(members, fields, levels, lat_cells),
            shape(members, fields, levels, lat_cells),
            shape(members, width, lat_cells),
            shape(3, width, lat_cells),
            jax.ShapeDtypeStruct((levels, lat_cells), jnp.int32),
            shape(members, 2, 2, levels, lat_cells),
        ),
        in_specs=[smem, vmem, vmem, smem, smem, vmem, smem, vmem, vmem],
        scratch_shapes=[pltpu.VMEM((fields, 8, levels, lat_cells), f32)],
        name="interior",
        compiler_params=room,
    )(parity, state, near, diffusion, radius, obs_cells, obs_count, obs_value, obs_error)
    far_b = lax.ppermute(far_b, "space", beyond_pairs)
    edge, winds, grid = pl.pallas_call(
        far_kernel,
        out_shape=(
            shape(members, 3, 2, levels, lat_cells),
            shape(members, 2, levels, lat_cells),
            shape(members, width, lat_cells),
        ),
        in_specs=[smem, vmem, smem] + [vmem] * 6,
        scratch_shapes=[pltpu.VMEM((members, width, lat_cells), f32)],
        name="edges",
        compiler_params=room,
    )(parity, state, diffusion, far_a, once_one, pre_zero, pre_one, column, grids)
    beside = lax.ppermute(grid, "space", beside_pairs)
    beyond = lax.ppermute(grid, "space", beyond_pairs)
    rest = pl.pallas_call(
        far_rest_kernel,
        out_shape=shape(members, 2, 2, levels, lat_cells),
        in_specs=[smem, vmem, smem] + [vmem] * 6,
        name="edges_rest",
        compiler_params=room,
    )(parity, state, diffusion, far_a, far_b, once_one, pre_zero, pre_one, winds)
    sends = pl.pallas_call(
        weights_kernel,
        out_shape=shape(width, 88, lat_cells),
        in_specs=[smem] + [vmem] * 7,
        scratch_shapes=[
            pltpu.VMEM((members, 24, lat_cells), f32),
            pltpu.VMEM((members, reach + 1, 2, 24, lat_cells // 2), f32),
            pltpu.VMEM((members, len(radii), width, lat_cells), f32),
        ],
        name="weights",
        compiler_params=room,
    )(parity, level_radius, grid, beside, beyond, core, edge, rest)
    parts = lax.all_to_all(sends, "mem", 0, 0, tiled=True)
    share = pl.pallas_call(
        combine_kernel,
        out_shape=shape(width, 80, lat_cells),
        in_specs=[vmem] * 2,
        name="combine",
        compiler_params=room,
    )(level_radius, parts)
    mean = lax.all_to_all(share, "mem", 0, 0, tiled=True)
    return pl.pallas_call(
        blend_kernel,
        out_shape=shape(*state.shape),
        in_specs=[smem] + [vmem] * 4,
        out_specs=anywhere,
        scratch_shapes=[pltpu.VMEM(state.shape, f32), pltpu.SemaphoreType.DMA((members, 2))],
        name="blend",
        compiler_params=room,
    )(parity, mean, core, edge, rest)


def solution(mesh):
    return jax.shard_map(
        local,
        mesh=mesh,
        in_specs=(
            P("mem", None, "space", None, None),
            P(),
            P(),
            P("space", None),
            P("space"),
            P("space", None),
            P("space", None),
        ),
        out_specs=P("mem", None, "space", None, None),
        check_vma=False,
    )
```

```python
import jax
import jax.numpy as jnp
import numpy as np
from jax import lax
from jax.experimental import pallas as pl
from jax.experimental.pallas import tpu as pltpu
from jax.sharding import PartitionSpec as P

time_step = 0.2
blend_share = 0.5
radii = (4, 5, 6, 7, 8)
reach = 7
f32 = jnp.float32
anywhere = pl.BlockSpec(memory_space=pl.ANY)
smem = pl.BlockSpec(memory_space=pltpu.SMEM)
vmem = pl.BlockSpec(memory_space=pltpu.VMEM)
room = pltpu.CompilerParams(vmem_limit_bytes=16 << 20)


def taper_of(distance_sq, radius):
    inverse = np.float32(1.0) / np.float32(radius * radius)
    share = max(np.float32(0.0), np.float32(1.0) - np.float32(distance_sq) * inverse)
    return float(np.float32(share * share))


def step_row(centre, west, east, u_part, v_part, rate):
    size = centre.shape[-1]
    north = pltpu.roll(centre, size - 1, 1)
    south = pltpu.roll(centre, 1, 1)
    spread = (east + west) + (north + south) - 4.0 * centre
    return centre + (rate * spread - (u_part * (east - west) + v_part * (north - south)))


def natural(row, parity):
    return row + parity * (7 - 2 * row)


def step_inner(centre, inner, u_part, v_part, rate):
    size = centre.shape[-1]
    north = pltpu.roll(centre, size - 1, 1)
    south = pltpu.roll(centre, 1, 1)
    spread = inner + (north + south) - 4.0 * centre
    return centre + (rate * spread - (u_part * inner + v_part * (north - south)))


def interior_kernel(
    parity_ref, state, near, diffusion, radius, cells, count, value, error,
    core, once_one, pre_zero, pre_one, column, grids, level_radius, far, once,
):
    sites = cells.shape[1]
    lat_cells = state.shape[4]
    parity = parity_ref[0]
    half = 0.5 * time_step
    signed = half * (1 - 2 * parity).astype(f32)
    far_start = 6 * parity

    def member(m, carry):
        def at(f, k):
            if k < 8:
                return state[m, f, natural(k, parity)]
            return near[m, f, parity if k == 8 else 1 - parity]

        for k in range(1, 9):
            u_part, v_part = signed * at(0, k), half * at(1, k)
            for f in range(5):
                once[f, k - 1] = step_row(
                    at(f, k), at(f, k - 1), at(f, k + 1), u_part, v_part, diffusion[f] * time_step
                )
        u_part, v_part = signed * at(0, 0), half * at(1, 0)
        for f in range(5):
            pre_zero[m, f] = step_inner(at(f, 0), at(f, 1), u_part, v_part, diffusion[f] * time_step)
        u_part, v_part = signed * once[0, 0], half * once[1, 0]
        for f in range(5):
            pre_one[m, f] = step_inner(once[f, 0], once[f, 1], u_part, v_part, diffusion[f] * time_step)
            once_one[m, f] = once[f, 0]
        column[m] = jnp.zeros((8, lat_cells), f32)
        for k in range(2, 8):
            u_part, v_part = signed * once[0, k - 1], half * once[1, k - 1]
            for f in range(5):
                row = step_row(
                    once[f, k - 1], once[f, k - 2], once[f, k], u_part, v_part, diffusion[f] * time_step
                )
                core[m, f, k - 2] = row
                if f == 2:
                    column[m, pl.ds(natural(k, parity), 1)] = jnp.mean(row, axis=0, keepdims=True)
        for f in (3, 4):
            for k in range(2):
                far[m, f - 3, k] = state[m, f, far_start + k]
        return carry

    lax.fori_loop(0, state.shape[0], member, 0)

    cell = cells[...]
    site_x = cell // lat_cells
    site_y = cell % lat_cells
    valid = lax.broadcasted_iota(jnp.int32, (1, sites), 1) < count[0]
    weight = jnp.where(valid, 1.0 / (error[...] * error[...]), 0.0)
    moments = jnp.concatenate([weight, weight * value[...], weight * value[...] * value[...]], axis=0)
    at_x = lax.broadcasted_iota(jnp.int32, (8, sites), 0) == site_x
    at_y = (lax.broadcasted_iota(jnp.int32, (lat_cells, sites), 0) == site_y).astype(f32)
    stacked = jnp.concatenate(
        [jnp.where(at_x, moments[k : k + 1], 0.0) for k in range(3)], axis=0
    )
    sums = lax.dot_general(
        stacked, at_y, (((1,), (1,)), ((), ())), precision=lax.Precision.HIGHEST, preferred_element_type=f32
    )
    total, first, second = sums[0:8], sums[8:16], sums[16:24]
    mean = jnp.where(total > 0.0, first / jnp.where(total > 0.0, total, 1.0), 0.0)
    grids[0] = total
    grids[1] = mean
    grids[2] = second - first * mean
    levels = level_radius.shape[0]
    level = lax.broadcasted_iota(jnp.int32, (levels, lat_cells), 0)
    chosen = jnp.full((levels, lat_cells), radius[0], jnp.int32)
    for z in range(1, levels):
        chosen = jnp.where(level == z, radius[z], chosen)
    level_radius[...] = chosen


def far_rows(beyond, next_to, zero, once_one, pre_zero, pre_one, winds, rate):
    (u_beyond, v_beyond), (u_zero, _), (u_one, _) = winds
    outside = step_row(next_to, beyond, zero, u_beyond, v_beyond, rate)
    first = pre_zero + next_to * (rate + u_zero)

    def again(u_part, v_part):
        return (
            step_row(first, outside, once_one, u_part, v_part, rate),
            pre_one + first * (rate + u_one),
        )

    return first, again


def far_winds(m, parity, state, far, once_one):
    half = 0.5 * time_step
    signed = half * (1 - 2 * parity).astype(f32)
    row = natural(0, parity)
    return (
        (signed * far[m, 0, 1 - parity], half * far[m, 1, 1 - parity]),
        (signed * state[m, 0, row], None),
        (signed * once_one[m, 0], None),
    )


def far_kernel(
    parity_ref, state, diffusion, far, once_one, pre_zero, pre_one, column, grids, edge, winds_out, grid, full
):
    parity = parity_ref[0]
    half = 0.5 * time_step
    signed = half * (1 - 2 * parity).astype(f32)

    def member(m, carry):
        winds = far_winds(m, parity, state, far, once_one)
        pairs = [
            far_rows(
                far[m, f, parity], far[m, f, 1 - parity], state[m, f, natural(0, parity)],
                once_one[m, f], pre_zero[m, f], pre_one[m, f], winds, diffusion[f] * time_step,
            )
            for f in range(3)
        ]
        u_part, v_part = signed * pairs[0][0], half * pairs[1][0]
        winds_out[m, 0] = u_part
        winds_out[m, 1] = v_part
        full[m] = column[m]
        for f in (2, 0, 1):
            for k, row in enumerate(pairs[f][1](u_part, v_part)):
                edge[m, f, k] = row
                if f == 2:
                    full[m, pl.ds(natural(k, parity), 1)] = jnp.mean(row, axis=0, keepdims=True)
        off = full[m] - grids[1]
        grid[m] = grids[0] * (off * off) + grids[2]
        return carry

    lax.fori_loop(0, state.shape[0], member, 0, unroll=True)


def far_rest_kernel(parity_ref, state, diffusion, far_winds_ref, far, once_one, pre_zero, pre_one, winds_in, edge):
    parity = parity_ref[0]

    def member(m, carry):
        winds = far_winds(m, parity, state, far_winds_ref, once_one)
        for f in (3, 4):
            _, again = far_rows(
                far[m, f - 3, parity], far[m, f - 3, 1 - parity], state[m, f, natural(0, parity)],
                once_one[m, f], pre_zero[m, f], pre_one[m, f], winds, diffusion[f] * time_step,
            )
            for k, row in enumerate(again(winds_in[m, 0], winds_in[m, 1])):
                edge[m, f - 3, k] = row
        return carry

    lax.fori_loop(0, state.shape[0], member, 0, unroll=True)


def by_level(rows, level_radius):
    result = jnp.broadcast_to(rows[0], level_radius.shape)
    for k in range(1, len(radii)):
        result = jnp.where(level_radius == radii[k], rows[k], result)
    return result


def final_row(m, f, k, core, edge, rest):
    if k >= 2:
        return core[m, f, k - 2]
    return edge[m, f, k] if f < 3 else rest[m, f - 3, k]


def weights_kernel(parity_ref, level_radius, own, beside, beyond, core, edge, rest, sends, near, shifted, expo):
    members, width, lat_cells = own.shape
    half = lat_cells // 2
    parity = parity_ref[0]

    def convolve(m, carry):
        near[m, pl.ds(16 * parity, 8)] = beyond[m]
        near[m, 8:16] = own[m]
        near[m, pl.ds(16 * (1 - parity), 8)] = beside[m]
        grid = near[m]
        for h in range(2):
            shifted[m, 0, h] = grid[:, half * h : half * h + half]
        for dy in range(1, reach + 1):
            both = pltpu.roll(grid, dy, 1) + pltpu.roll(grid, lat_cells - dy, 1)
            for h in range(2):
                shifted[m, dy, h] = both[:, half * h : half * h + half]
        for h in range(2):
            sums = [None] * len(radii)
            for dx in range(reach + 1):
                for dy in range(reach + 1):
                    distance_sq = dx * dx + dy * dy
                    if distance_sq >= radii[-1] ** 2:
                        continue
                    if dx == 0:
                        pair = shifted[m, dy, h, 8:16]
                    else:
                        pair = shifted[m, dy, h, 8 + dx : 16 + dx] + shifted[m, dy, h, 8 - dx : 16 - dx]
                    for k, radius in enumerate(radii):
                        if distance_sq < radius * radius:
                            term = pair * (-0.5 * taper_of(distance_sq, radius))
                            sums[k] = term if sums[k] is None else sums[k] + term
            for k in range(len(radii)):
                expo[m, k, :, half * h : half * h + half] = sums[k]
        return carry

    lax.fori_loop(0, members, convolve, 0, unroll=True)
    for k in range(len(radii)):
        logs = [expo[m, k] for m in range(members)]
        best = logs[0]
        for m in range(1, members):
            best = jnp.maximum(best, logs[m])
        values = [jnp.exp(logs[m] - best) for m in range(members)]
        total = values[0]
        for m in range(1, members):
            total = total + values[m]
        over = 1.0 / total
        for m in range(members):
            expo[m, k] = values[m] * over
        level_log = best + jnp.log(total)
        for x in range(width):
            sends[natural(x, parity), 80 + k : 81 + k] = level_log[x : x + 1]
    for x in range(width):
        here = pl.ds(natural(x, parity), 1)
        sends[x, 85:88] = jnp.zeros((3, lat_cells), f32)
        sums = [None] * 5
        for m in range(members):
            weight = by_level([expo[m, k, here] for k in range(len(radii))], level_radius[...])
            for f in range(5):
                row = final_row(m, f, x, core, edge, rest)
                term = weight * row
                sums[f] = term if sums[f] is None else sums[f] + term
        for f in range(5):
            sends[x, 16 * f : 16 * f + 16] = sums[f]


def combine_kernel(level_radius, parts, result):
    sources = parts.shape[0]
    logs = [parts[d, 80:85] for d in range(sources)]
    best = logs[0]
    for d in range(1, sources):
        best = jnp.maximum(best, logs[d])
    scales = [jnp.exp(logs[d] - best) for d in range(sources)]
    total = scales[0]
    for d in range(1, sources):
        total = total + scales[d]
    over = 1.0 / total
    sums = [None] * 5
    for d in range(sources):
        share = scales[d] * over
        weight = by_level([share[k : k + 1] for k in range(len(radii))], level_radius[...])
        for f in range(5):
            term = weight * parts[d, 16 * f : 16 * f + 16]
            sums[f] = term if sums[f] is None else sums[f] + term
    for f in range(5):
        for d in range(sources):
            result[d, 16 * f : 16 * f + 16] = sums[f]


def blend_kernel(parity_ref, mean, core, edge, rest, out, done, sems):
    members = core.shape[0]
    parity = parity_ref[0]
    copies = []
    for m in range(members):
        for part in range(2):
            for k in range(4 * part, 4 * part + 4):
                for f in range(5):
                    row = final_row(m, f, k, core, edge, rest)
                    done[m, f, natural(k, parity)] = row + blend_share * (mean[k, 16 * f : 16 * f + 16] - row)
            rows = pl.ds(4 * (part + parity * (1 - 2 * part)), 4)
            copy = pltpu.make_async_copy(done.at[m, :, rows], out.at[m, :, rows], sems.at[m, part])
            copy.start()
            copies.append(copy)
    for copy in copies:
        copy.wait()


def local(state, diffusion, radius, obs_cells, obs_count, obs_value, obs_error):
    members, fields, width, levels, lat_cells = state.shape
    size = lax.axis_size("space")
    parity = (lax.axis_index("space") & 1).astype(jnp.int32).reshape(1)
    beside_pairs = [(i, i + 1 - 2 * (i % 2)) for i in range(size)]
    beyond_pairs = [(i, (i - 1 + 2 * (i % 2)) % size) for i in range(size)]

    orders = ((0, 2, 4, 6, 1, 3, 5, 7), (6, 4, 2, 0, 7, 5, 3, 1))
    groups = [[m * size + t for m in orders[t % 2]] for t in range(size)]

    def shape(*dims):
        return jax.ShapeDtypeStruct(dims, f32)

    near = lax.dynamic_slice_in_dim(state, 6 * (1 - parity[0]), 2, axis=2)
    far_a = lax.dynamic_slice_in_dim(state[:, :3], 6 * parity[0], 2, axis=2)
    near = lax.ppermute(near, "space", beside_pairs)
    far_a = lax.ppermute(far_a, "space", beyond_pairs)
    core, once_one, pre_zero, pre_one, column, grids, level_radius, far_b = pl.pallas_call(
        interior_kernel,
        out_shape=(
            shape(members, fields, 6, levels, lat_cells),
            shape(members, fields, levels, lat_cells),
            shape(members, fields, levels, lat_cells),
            shape(members, fields, levels, lat_cells),
            shape(members, width, lat_cells),
            shape(3, width, lat_cells),
            jax.ShapeDtypeStruct((levels, lat_cells), jnp.int32),
            shape(members, 2, 2, levels, lat_cells),
        ),
        in_specs=[smem, vmem, vmem, smem, smem, vmem, smem, vmem, vmem],
        scratch_shapes=[pltpu.VMEM((fields, 8, levels, lat_cells), f32)],
        name="interior",
        compiler_params=room,
    )(parity, state, near, diffusion, radius, obs_cells, obs_count, obs_value, obs_error)
    far_b = lax.ppermute(far_b, "space", beyond_pairs)
    edge, winds, grid = pl.pallas_call(
        far_kernel,
        out_shape=(
            shape(members, 3, 2, levels, lat_cells),
            shape(members, 2, levels, lat_cells),
            shape(members, width, lat_cells),
        ),
        in_specs=[smem, vmem, smem] + [vmem] * 6,
        scratch_shapes=[pltpu.VMEM((members, width, lat_cells), f32)],
        name="edges",
        compiler_params=room,
    )(parity, state, diffusion, far_a, once_one, pre_zero, pre_one, column, grids)
    beside = lax.ppermute(grid, "space", beside_pairs)
    beyond = lax.ppermute(grid, "space", beyond_pairs)
    rest = pl.pallas_call(
        far_rest_kernel,
        out_shape=shape(members, 2, 2, levels, lat_cells),
        in_specs=[smem, vmem, smem] + [vmem] * 6,
        name="edges_rest",
        compiler_params=room,
    )(parity, state, diffusion, far_a, far_b, once_one, pre_zero, pre_one, winds)
    sends = pl.pallas_call(
        weights_kernel,
        out_shape=shape(width, 88, lat_cells),
        in_specs=[smem] + [vmem] * 7,
        scratch_shapes=[
            pltpu.VMEM((members, 24, lat_cells), f32),
            pltpu.VMEM((members, reach + 1, 2, 24, lat_cells // 2), f32),
            pltpu.VMEM((members, len(radii), width, lat_cells), f32),
        ],
        name="weights",
        compiler_params=room,
    )(parity, level_radius, grid, beside, beyond, core, edge, rest)
    parts = lax.all_to_all(sends, ("mem", "space"), 0, 0, tiled=True, axis_index_groups=groups)
    share = pl.pallas_call(
        combine_kernel,
        out_shape=shape(width, 80, lat_cells),
        in_specs=[vmem] * 2,
        name="combine",
        compiler_params=room,
    )(level_radius, parts)
    mean = lax.all_to_all(share, ("mem", "space"), 0, 0, tiled=True, axis_index_groups=groups)
    return pl.pallas_call(
        blend_kernel,
        out_shape=shape(*state.shape),
        in_specs=[smem] + [vmem] * 4,
        out_specs=anywhere,
        scratch_shapes=[pltpu.VMEM(state.shape, f32), pltpu.SemaphoreType.DMA((members, 2))],
        name="blend",
        compiler_params=room,
    )(parity, mean, core, edge, rest)


def solution(mesh):
    return jax.shard_map(
        local,
        mesh=mesh,
        in_specs=(
            P("mem", None, "space", None, None),
            P(),
            P(),
            P("space", None),
            P("space"),
            P("space", None),
            P("space", None),
        ),
        out_specs=P("mem", None, "space", None, None),
        check_vma=False,
    )
```

```python
import jax
import jax.numpy as jnp
import numpy as np
from jax import lax
from jax.experimental import pallas as pl
from jax.experimental.pallas import tpu as pltpu
from jax.sharding import PartitionSpec as P

time_step = 0.2
blend_share = 0.5
radii = (4, 5, 6, 7, 8)
reach = 7
f32 = jnp.float32
anywhere = pl.BlockSpec(memory_space=pl.ANY)
smem = pl.BlockSpec(memory_space=pltpu.SMEM)
vmem = pl.BlockSpec(memory_space=pltpu.VMEM)
room = pltpu.CompilerParams(vmem_limit_bytes=16 << 20)


def taper_of(distance_sq, radius):
    inverse = np.float32(1.0) / np.float32(radius * radius)
    share = max(np.float32(0.0), np.float32(1.0) - np.float32(distance_sq) * inverse)
    return float(np.float32(share * share))


def step_row(centre, west, east, u_part, v_part, rate):
    size = centre.shape[-1]
    north = pltpu.roll(centre, size - 1, 1)
    south = pltpu.roll(centre, 1, 1)
    spread = (east + west) + (north + south) - 4.0 * centre
    return centre + (rate * spread - (u_part * (east - west) + v_part * (north - south)))


def natural(row, parity):
    return row + parity * (7 - 2 * row)


def step_inner(centre, inner, u_part, v_part, rate):
    size = centre.shape[-1]
    north = pltpu.roll(centre, size - 1, 1)
    south = pltpu.roll(centre, 1, 1)
    spread = inner + (north + south) - 4.0 * centre
    return centre + (rate * spread - (u_part * inner + v_part * (north - south)))


def interior_kernel(
    state, near, diffusion, radius, cells, count, value, error,
    core, once_one, pre_zero, pre_one, column, grids, level_radius, far, rates, once,
):
    sites = cells.shape[1]
    lat_cells = state.shape[4]
    parity = lax.rem(lax.axis_index("space"), 2)
    half = 0.5 * time_step
    signed = half * (1 - 2 * parity).astype(f32)
    far_start = 6 * parity

    def member(m, carry):
        def at(f, k):
            if k < 8:
                return state[m, f, natural(k, parity)]
            return near[m, f, parity if k == 8 else 1 - parity]

        for k in range(1, 9):
            u_part, v_part = signed * at(0, k), half * at(1, k)
            for f in range(5):
                once[f, k - 1] = step_row(
                    at(f, k), at(f, k - 1), at(f, k + 1), u_part, v_part, diffusion[f] * time_step
                )
        u_part, v_part = signed * at(0, 0), half * at(1, 0)
        for f in range(5):
            pre_zero[m, f] = step_inner(at(f, 0), at(f, 1), u_part, v_part, diffusion[f] * time_step)
        u_part, v_part = signed * once[0, 0], half * once[1, 0]
        for f in range(5):
            pre_one[m, f] = step_inner(once[f, 0], once[f, 1], u_part, v_part, diffusion[f] * time_step)
            once_one[m, f] = once[f, 0]
        column[m] = jnp.zeros((8, lat_cells), f32)
        for k in range(2, 8):
            u_part, v_part = signed * once[0, k - 1], half * once[1, k - 1]
            for f in range(5):
                row = step_row(
                    once[f, k - 1], once[f, k - 2], once[f, k], u_part, v_part, diffusion[f] * time_step
                )
                core[m, f, k - 2] = row
                if f == 2:
                    column[m, pl.ds(natural(k, parity), 1)] = jnp.mean(row, axis=0, keepdims=True)
        for f in (3, 4):
            for k in range(2):
                far[m, f - 3, k] = state[m, f, far_start + k]
        return carry

    lax.fori_loop(0, state.shape[0], member, 0)

    cell = cells[...]
    site_x = cell // lat_cells
    site_y = cell % lat_cells
    valid = lax.broadcasted_iota(jnp.int32, (1, sites), 1) < count[0]
    weight = jnp.where(valid, 1.0 / (error[...] * error[...]), 0.0)
    moments = jnp.concatenate([weight, weight * value[...], weight * value[...] * value[...]], axis=0)
    at_x = lax.broadcasted_iota(jnp.int32, (8, sites), 0) == site_x
    at_y = (lax.broadcasted_iota(jnp.int32, (lat_cells, sites), 0) == site_y).astype(f32)
    stacked = jnp.concatenate(
        [jnp.where(at_x, moments[k : k + 1], 0.0) for k in range(3)], axis=0
    )
    sums = lax.dot_general(
        stacked, at_y, (((1,), (1,)), ((), ())), precision=lax.Precision.HIGHEST, preferred_element_type=f32
    )
    total, first, second = sums[0:8], sums[8:16], sums[16:24]
    mean = jnp.where(total > 0.0, first / jnp.where(total > 0.0, total, 1.0), 0.0)
    grids[0] = total
    grids[1] = mean
    grids[2] = second - first * mean
    for f in range(5):
        rates[f : f + 1] = jnp.full((1, lat_cells), diffusion[f] * time_step, f32)
    rates[5:8] = jnp.zeros((3, lat_cells), f32)
    levels = level_radius.shape[0]
    level = lax.broadcasted_iota(jnp.int32, (levels, lat_cells), 0)
    chosen = jnp.full((levels, lat_cells), radius[0], jnp.int32)
    for z in range(1, levels):
        chosen = jnp.where(level == z, radius[z], chosen)
    level_radius[...] = chosen


def far_rows(beyond, next_to, zero, once_one, pre_zero, pre_one, winds, rate):
    (u_beyond, v_beyond), (u_zero, _), (u_one, _) = winds
    outside = step_row(next_to, beyond, zero, u_beyond, v_beyond, rate)
    first = pre_zero + next_to * (rate + u_zero)

    def again(u_part, v_part):
        return (
            step_row(first, outside, once_one, u_part, v_part, rate),
            pre_one + first * (rate + u_one),
        )

    return first, again


def far_winds(m, parity, state, far, once_one):
    half = 0.5 * time_step
    signed = half * (1 - 2 * parity).astype(f32)
    row = natural(0, parity)
    return (
        (signed * far[m, 0, 1 - parity], half * far[m, 1, 1 - parity]),
        (signed * state[m, 0, row], None),
        (signed * once_one[m, 0], None),
    )


def far_kernel(
    state, rates, far, once_one, pre_zero, pre_one, column, grids, edge, winds_out, grid, full
):
    parity = lax.rem(lax.axis_index("space"), 2)
    half = 0.5 * time_step
    signed = half * (1 - 2 * parity).astype(f32)

    def member(m, carry):
        winds = far_winds(m, parity, state, far, once_one)
        pairs = [
            far_rows(
                far[m, f, parity], far[m, f, 1 - parity], state[m, f, natural(0, parity)],
                once_one[m, f], pre_zero[m, f], pre_one[m, f], winds, rates[f : f + 1],
            )
            for f in range(3)
        ]
        u_part, v_part = signed * pairs[0][0], half * pairs[1][0]
        winds_out[m, 0] = u_part
        winds_out[m, 1] = v_part
        full[m] = column[m]
        for f in (2, 0, 1):
            for k, row in enumerate(pairs[f][1](u_part, v_part)):
                edge[m, f, k] = row
                if f == 2:
                    full[m, pl.ds(natural(k, parity), 1)] = jnp.mean(row, axis=0, keepdims=True)
        off = full[m] - grids[1]
        grid[m] = grids[0] * (off * off) + grids[2]
        return carry

    lax.fori_loop(0, state.shape[0], member, 0, unroll=True)


def far_rest_kernel(state, rates, far_winds_ref, far, once_one, pre_zero, pre_one, winds_in, edge):
    parity = lax.rem(lax.axis_index("space"), 2)

    def member(m, carry):
        winds = far_winds(m, parity, state, far_winds_ref, once_one)
        for f in (3, 4):
            _, again = far_rows(
                far[m, f - 3, parity], far[m, f - 3, 1 - parity], state[m, f, natural(0, parity)],
                once_one[m, f], pre_zero[m, f], pre_one[m, f], winds, rates[f : f + 1],
            )
            for k, row in enumerate(again(winds_in[m, 0], winds_in[m, 1])):
                edge[m, f - 3, k] = row
        return carry

    lax.fori_loop(0, state.shape[0], member, 0, unroll=True)


def by_level(rows, level_radius):
    result = jnp.broadcast_to(rows[0], level_radius.shape)
    for k in range(1, len(radii)):
        result = jnp.where(level_radius == radii[k], rows[k], result)
    return result


def final_row(m, f, k, core, edge, rest):
    if k >= 2:
        return core[m, f, k - 2]
    return edge[m, f, k] if f < 3 else rest[m, f - 3, k]


def weights_kernel(level_radius, own, beside, beyond, core, edge, rest, sends, near, shifted, expo):
    members, width, lat_cells = own.shape
    half = lat_cells // 2
    parity = lax.rem(lax.axis_index("space"), 2)

    def convolve(m, carry):
        near[m, pl.ds(16 * parity, 8)] = beyond[m]
        near[m, 8:16] = own[m]
        near[m, pl.ds(16 * (1 - parity), 8)] = beside[m]
        grid = near[m]
        for h in range(2):
            shifted[m, 0, h] = grid[:, half * h : half * h + half]
        for dy in range(1, reach + 1):
            both = pltpu.roll(grid, dy, 1) + pltpu.roll(grid, lat_cells - dy, 1)
            for h in range(2):
                shifted[m, dy, h] = both[:, half * h : half * h + half]
        for h in range(2):
            sums = [None] * len(radii)
            for dx in range(reach + 1):
                for dy in range(reach + 1):
                    distance_sq = dx * dx + dy * dy
                    if distance_sq >= radii[-1] ** 2:
                        continue
                    if dx == 0:
                        pair = shifted[m, dy, h, 8:16]
                    else:
                        pair = shifted[m, dy, h, 8 + dx : 16 + dx] + shifted[m, dy, h, 8 - dx : 16 - dx]
                    for k, radius in enumerate(radii):
                        if distance_sq < radius * radius:
                            term = pair * (-0.5 * taper_of(distance_sq, radius))
                            sums[k] = term if sums[k] is None else sums[k] + term
            for k in range(len(radii)):
                expo[m, k, :, half * h : half * h + half] = sums[k]
        return carry

    lax.fori_loop(0, members, convolve, 0, unroll=True)
    for k in range(len(radii)):
        logs = [expo[m, k] for m in range(members)]
        best = logs[0]
        for m in range(1, members):
            best = jnp.maximum(best, logs[m])
        values = [jnp.exp(logs[m] - best) for m in range(members)]
        total = values[0]
        for m in range(1, members):
            total = total + values[m]
        over = 1.0 / total
        for m in range(members):
            expo[m, k] = values[m] * over
        level_log = best + jnp.log(total)
        for x in range(width):
            sends[natural(x, parity), 80 + k : 81 + k] = level_log[x : x + 1]
    for x in range(width):
        here = pl.ds(natural(x, parity), 1)
        sends[x, 85:88] = jnp.zeros((3, lat_cells), f32)
        sums = [None] * 5
        for m in range(members):
            weight = by_level([expo[m, k, here] for k in range(len(radii))], level_radius[...])
            for f in range(5):
                row = final_row(m, f, x, core, edge, rest)
                term = weight * row
                sums[f] = term if sums[f] is None else sums[f] + term
        for f in range(5):
            sends[x, 16 * f : 16 * f + 16] = sums[f]


def combine_kernel(level_radius, parts, result):
    sources = parts.shape[0]
    logs = [parts[d, 80:85] for d in range(sources)]
    best = logs[0]
    for d in range(1, sources):
        best = jnp.maximum(best, logs[d])
    scales = [jnp.exp(logs[d] - best) for d in range(sources)]
    total = scales[0]
    for d in range(1, sources):
        total = total + scales[d]
    over = 1.0 / total
    sums = [None] * 5
    for d in range(sources):
        share = scales[d] * over
        weight = by_level([share[k : k + 1] for k in range(len(radii))], level_radius[...])
        for f in range(5):
            term = weight * parts[d, 16 * f : 16 * f + 16]
            sums[f] = term if sums[f] is None else sums[f] + term
    for f in range(5):
        for d in range(sources):
            result[d, 16 * f : 16 * f + 16] = sums[f]


def blend_kernel(mean, core, edge, rest, out, done, sems):
    members = core.shape[0]
    parity = lax.rem(lax.axis_index("space"), 2)
    copies = []
    for m in range(members):
        for part in range(2):
            for k in range(4 * part, 4 * part + 4):
                for f in range(5):
                    row = final_row(m, f, k, core, edge, rest)
                    done[m, f, natural(k, parity)] = row + blend_share * (mean[k, 16 * f : 16 * f + 16] - row)
            rows = pl.ds(4 * (part + parity * (1 - 2 * part)), 4)
            copy = pltpu.make_async_copy(done.at[m, :, rows], out.at[m, :, rows], sems.at[m, part])
            copy.start()
            copies.append(copy)
    for copy in copies:
        copy.wait()


def local(state, diffusion, radius, obs_cells, obs_count, obs_value, obs_error):
    members, fields, width, levels, lat_cells = state.shape
    size = lax.axis_size("space")
    parity = (lax.axis_index("space") & 1).astype(jnp.int32).reshape(1)
    beside_pairs = [(i, i + 1 - 2 * (i % 2)) for i in range(size)]
    beyond_pairs = [(i, (i - 1 + 2 * (i % 2)) % size) for i in range(size)]

    orders = ((0, 2, 4, 6, 1, 3, 5, 7), (6, 4, 2, 0, 7, 5, 3, 1))
    groups = [[m * size + t for m in orders[t % 2]] for t in range(size)]

    def shape(*dims):
        return jax.ShapeDtypeStruct(dims, f32)

    near = lax.dynamic_slice_in_dim(state, 6 * (1 - parity[0]), 2, axis=2)
    far_a = lax.dynamic_slice_in_dim(state[:, :3], 6 * parity[0], 2, axis=2)
    near = lax.ppermute(near, "space", beside_pairs)
    far_a = lax.ppermute(far_a, "space", beyond_pairs)
    core, once_one, pre_zero, pre_one, column, grids, level_radius, far_b, rates = pl.pallas_call(
        interior_kernel,
        out_shape=(
            shape(members, fields, 6, levels, lat_cells),
            shape(members, fields, levels, lat_cells),
            shape(members, fields, levels, lat_cells),
            shape(members, fields, levels, lat_cells),
            shape(members, width, lat_cells),
            shape(3, width, lat_cells),
            jax.ShapeDtypeStruct((levels, lat_cells), jnp.int32),
            shape(members, 2, 2, levels, lat_cells),
            shape(8, lat_cells),
        ),
        in_specs=[vmem, vmem, smem, smem, vmem, smem, vmem, vmem],
        scratch_shapes=[pltpu.VMEM((fields, 8, levels, lat_cells), f32)],
        name="interior",
        compiler_params=room,
    )(state, near, diffusion, radius, obs_cells, obs_count, obs_value, obs_error)
    far_b = lax.ppermute(far_b, "space", beyond_pairs)
    edge, winds, grid = pl.pallas_call(
        far_kernel,
        out_shape=(
            shape(members, 3, 2, levels, lat_cells),
            shape(members, 2, levels, lat_cells),
            shape(members, width, lat_cells),
        ),
        in_specs=[vmem] * 8,
        scratch_shapes=[pltpu.VMEM((members, width, lat_cells), f32)],
        name="edges",
        compiler_params=room,
    )(state, rates, far_a, once_one, pre_zero, pre_one, column, grids)
    beside = lax.ppermute(grid, "space", beside_pairs)
    beyond = lax.ppermute(grid, "space", beyond_pairs)
    rest = pl.pallas_call(
        far_rest_kernel,
        out_shape=shape(members, 2, 2, levels, lat_cells),
        in_specs=[vmem] * 8,
        name="edges_rest",
        compiler_params=room,
    )(state, rates, far_a, far_b, once_one, pre_zero, pre_one, winds)
    sends = pl.pallas_call(
        weights_kernel,
        out_shape=shape(width, 88, lat_cells),
        in_specs=[vmem] * 7,
        scratch_shapes=[
            pltpu.VMEM((members, 24, lat_cells), f32),
            pltpu.VMEM((members, reach + 1, 2, 24, lat_cells // 2), f32),
            pltpu.VMEM((members, len(radii), width, lat_cells), f32),
        ],
        name="weights",
        compiler_params=room,
    )(level_radius, grid, beside, beyond, core, edge, rest)
    parts = lax.all_to_all(sends, ("mem", "space"), 0, 0, tiled=True, axis_index_groups=groups)
    share = pl.pallas_call(
        combine_kernel,
        out_shape=shape(width, 80, lat_cells),
        in_specs=[vmem] * 2,
        name="combine",
        compiler_params=room,
    )(level_radius, parts)
    mean = lax.all_to_all(share, ("mem", "space"), 0, 0, tiled=True, axis_index_groups=groups)
    return pl.pallas_call(
        blend_kernel,
        out_shape=shape(*state.shape),
        in_specs=[vmem] * 4,
        out_specs=anywhere,
        scratch_shapes=[pltpu.VMEM(state.shape, f32), pltpu.SemaphoreType.DMA((members, 2))],
        name="blend",
        compiler_params=room,
    )(mean, core, edge, rest)


def solution(mesh):
    return jax.shard_map(
        local,
        mesh=mesh,
        in_specs=(
            P("mem", None, "space", None, None),
            P(),
            P(),
            P("space", None),
            P("space"),
            P("space", None),
            P("space", None),
        ),
        out_specs=P("mem", None, "space", None, None),
        check_vma=False,
    )
```

```python
import jax
import jax.numpy as jnp
import numpy as np
from jax import lax
from jax.experimental import pallas as pl
from jax.experimental.pallas import tpu as pltpu
from jax.sharding import PartitionSpec as P

time_step = 0.2
blend_share = 0.5
radii = (4, 5, 6, 7, 8)
reach = 7
f32 = jnp.float32
anywhere = pl.BlockSpec(memory_space=pl.ANY)
smem = pl.BlockSpec(memory_space=pltpu.SMEM)
vmem = pl.BlockSpec(memory_space=pltpu.VMEM)
room = pltpu.CompilerParams(vmem_limit_bytes=16 << 20)


def taper_of(distance_sq, radius):
    inverse = np.float32(1.0) / np.float32(radius * radius)
    share = max(np.float32(0.0), np.float32(1.0) - np.float32(distance_sq) * inverse)
    return float(np.float32(share * share))


def step_row(centre, west, east, u_part, v_part, rate):
    size = centre.shape[-1]
    north = pltpu.roll(centre, size - 1, 1)
    south = pltpu.roll(centre, 1, 1)
    spread = (east + west) + (north + south) - 4.0 * centre
    return centre + (rate * spread - (u_part * (east - west) + v_part * (north - south)))


def natural(row, parity):
    return row + parity * (7 - 2 * row)


def step_inner(centre, inner, u_part, v_part, rate):
    size = centre.shape[-1]
    north = pltpu.roll(centre, size - 1, 1)
    south = pltpu.roll(centre, 1, 1)
    spread = inner + (north + south) - 4.0 * centre
    return centre + (rate * spread - (u_part * inner + v_part * (north - south)))


def interior_kernel(
    state, near, diffusion, radius, cells, count, value, error,
    core, once_one, pre_zero, pre_one, column, grids, level_radius, far, rates, once,
):
    sites = cells.shape[1]
    lat_cells = state.shape[4]
    parity = lax.rem(lax.axis_index("space"), 2)
    half = 0.5 * time_step
    signed = half * (1 - 2 * parity).astype(f32)
    far_start = 6 * parity

    def member(m, carry):
        def at(f, k):
            if k < 8:
                return state[m, f, natural(k, parity)]
            return near[m, f, parity if k == 8 else 1 - parity]

        for k in range(1, 9):
            u_part, v_part = signed * at(0, k), half * at(1, k)
            for f in range(5):
                once[f, k - 1] = step_row(
                    at(f, k), at(f, k - 1), at(f, k + 1), u_part, v_part, diffusion[f] * time_step
                )
        u_part, v_part = signed * at(0, 0), half * at(1, 0)
        for f in range(5):
            pre_zero[m, f] = step_inner(at(f, 0), at(f, 1), u_part, v_part, diffusion[f] * time_step)
        u_part, v_part = signed * once[0, 0], half * once[1, 0]
        for f in range(5):
            pre_one[m, f] = step_inner(once[f, 0], once[f, 1], u_part, v_part, diffusion[f] * time_step)
            once_one[m, f] = once[f, 0]
        column[m] = jnp.zeros((8, lat_cells), f32)
        for k in range(2, 8):
            u_part, v_part = signed * once[0, k - 1], half * once[1, k - 1]
            for f in range(5):
                row = step_row(
                    once[f, k - 1], once[f, k - 2], once[f, k], u_part, v_part, diffusion[f] * time_step
                )
                core[m, f, k - 2] = row
                if f == 2:
                    column[m, pl.ds(natural(k, parity), 1)] = jnp.mean(row, axis=0, keepdims=True)
        for f in (3, 4):
            for k in range(2):
                far[m, f - 3, k] = state[m, f, far_start + k]
        return carry

    lax.fori_loop(0, state.shape[0], member, 0, unroll=True)

    cell = cells[...]
    site_x = cell // lat_cells
    site_y = cell % lat_cells
    valid = lax.broadcasted_iota(jnp.int32, (1, sites), 1) < count[0]
    weight = jnp.where(valid, 1.0 / (error[...] * error[...]), 0.0)
    moments = jnp.concatenate([weight, weight * value[...], weight * value[...] * value[...]], axis=0)
    at_x = lax.broadcasted_iota(jnp.int32, (8, sites), 0) == site_x
    at_y = (lax.broadcasted_iota(jnp.int32, (lat_cells, sites), 0) == site_y).astype(f32)
    stacked = jnp.concatenate(
        [jnp.where(at_x, moments[k : k + 1], 0.0) for k in range(3)], axis=0
    )
    sums = lax.dot_general(
        stacked, at_y, (((1,), (1,)), ((), ())), precision=lax.Precision.HIGHEST, preferred_element_type=f32
    )
    total, first, second = sums[0:8], sums[8:16], sums[16:24]
    mean = jnp.where(total > 0.0, first / jnp.where(total > 0.0, total, 1.0), 0.0)
    grids[0] = total
    grids[1] = mean
    grids[2] = second - first * mean
    for f in range(5):
        rates[f : f + 1] = jnp.full((1, lat_cells), diffusion[f] * time_step, f32)
    rates[5:8] = jnp.zeros((3, lat_cells), f32)
    levels = level_radius.shape[0]
    level = lax.broadcasted_iota(jnp.int32, (levels, lat_cells), 0)
    chosen = jnp.full((levels, lat_cells), radius[0], jnp.int32)
    for z in range(1, levels):
        chosen = jnp.where(level == z, radius[z], chosen)
    level_radius[...] = chosen


def far_rows(beyond, next_to, zero, once_one, pre_zero, pre_one, winds, rate):
    (u_beyond, v_beyond), (u_zero, _), (u_one, _) = winds
    outside = step_row(next_to, beyond, zero, u_beyond, v_beyond, rate)
    first = pre_zero + next_to * (rate + u_zero)

    def again(u_part, v_part):
        return (
            step_row(first, outside, once_one, u_part, v_part, rate),
            pre_one + first * (rate + u_one),
        )

    return first, again


def far_winds(m, parity, state, far, once_one):
    half = 0.5 * time_step
    signed = half * (1 - 2 * parity).astype(f32)
    row = natural(0, parity)
    return (
        (signed * far[m, 0, 1 - parity], half * far[m, 1, 1 - parity]),
        (signed * state[m, 0, row], None),
        (signed * once_one[m, 0], None),
    )


def far_kernel(
    state, rates, far, once_one, pre_zero, pre_one, column, grids, edge, winds_out, grid, full
):
    parity = lax.rem(lax.axis_index("space"), 2)
    half = 0.5 * time_step
    signed = half * (1 - 2 * parity).astype(f32)

    def member(m, carry):
        winds = far_winds(m, parity, state, far, once_one)
        pairs = [
            far_rows(
                far[m, f, parity], far[m, f, 1 - parity], state[m, f, natural(0, parity)],
                once_one[m, f], pre_zero[m, f], pre_one[m, f], winds, rates[f : f + 1],
            )
            for f in range(3)
        ]
        u_part, v_part = signed * pairs[0][0], half * pairs[1][0]
        winds_out[m, 0] = u_part
        winds_out[m, 1] = v_part
        full[m] = column[m]
        for f in (2, 0, 1):
            for k, row in enumerate(pairs[f][1](u_part, v_part)):
                edge[m, f, k] = row
                if f == 2:
                    full[m, pl.ds(natural(k, parity), 1)] = jnp.mean(row, axis=0, keepdims=True)
        off = full[m] - grids[1]
        grid[m] = grids[0] * (off * off) + grids[2]
        return carry

    lax.fori_loop(0, state.shape[0], member, 0, unroll=True)


def far_rest_kernel(state, rates, far_winds_ref, far, once_one, pre_zero, pre_one, winds_in, edge):
    parity = lax.rem(lax.axis_index("space"), 2)

    def member(m, carry):
        winds = far_winds(m, parity, state, far_winds_ref, once_one)
        for f in (3, 4):
            _, again = far_rows(
                far[m, f - 3, parity], far[m, f - 3, 1 - parity], state[m, f, natural(0, parity)],
                once_one[m, f], pre_zero[m, f], pre_one[m, f], winds, rates[f : f + 1],
            )
            for k, row in enumerate(again(winds_in[m, 0], winds_in[m, 1])):
                edge[m, f - 3, k] = row
        return carry

    lax.fori_loop(0, state.shape[0], member, 0, unroll=True)


def by_level(rows, level_radius):
    result = jnp.broadcast_to(rows[0], level_radius.shape)
    for k in range(1, len(radii)):
        result = jnp.where(level_radius == radii[k], rows[k], result)
    return result


def final_row(m, f, k, core, edge, rest):
    if k >= 2:
        return core[m, f, k - 2]
    return edge[m, f, k] if f < 3 else rest[m, f - 3, k]


def weights_kernel(level_radius, own, beside, beyond, core, edge, rest, sends, near, shifted, expo):
    members, width, lat_cells = own.shape
    half = lat_cells // 2
    parity = lax.rem(lax.axis_index("space"), 2)

    def convolve(m, carry):
        near[m, pl.ds(16 * parity, 8)] = beyond[m]
        near[m, 8:16] = own[m]
        near[m, pl.ds(16 * (1 - parity), 8)] = beside[m]
        grid = near[m]
        for h in range(2):
            shifted[m, 0, h] = grid[:, half * h : half * h + half]
        for dy in range(1, reach + 1):
            both = pltpu.roll(grid, dy, 1) + pltpu.roll(grid, lat_cells - dy, 1)
            for h in range(2):
                shifted[m, dy, h] = both[:, half * h : half * h + half]
        for h in range(2):
            sums = [None] * len(radii)
            for dx in range(reach + 1):
                for dy in range(reach + 1):
                    distance_sq = dx * dx + dy * dy
                    if distance_sq >= radii[-1] ** 2:
                        continue
                    if dx == 0:
                        pair = shifted[m, dy, h, 8:16]
                    else:
                        pair = shifted[m, dy, h, 8 + dx : 16 + dx] + shifted[m, dy, h, 8 - dx : 16 - dx]
                    for k, radius in enumerate(radii):
                        if distance_sq < radius * radius:
                            term = pair * (-0.5 * taper_of(distance_sq, radius))
                            sums[k] = term if sums[k] is None else sums[k] + term
            for k in range(len(radii)):
                expo[m, k, :, half * h : half * h + half] = sums[k]
        return carry

    lax.fori_loop(0, members, convolve, 0, unroll=True)
    for k in range(len(radii)):
        logs = [expo[m, k] for m in range(members)]
        best = logs[0]
        for m in range(1, members):
            best = jnp.maximum(best, logs[m])
        values = [jnp.exp(logs[m] - best) for m in range(members)]
        total = values[0]
        for m in range(1, members):
            total = total + values[m]
        over = 1.0 / total
        for m in range(members):
            expo[m, k] = values[m] * over
        level_log = best + jnp.log(total)
        for x in range(width):
            sends[natural(x, parity), 80 + k : 81 + k] = level_log[x : x + 1]
    for x in range(width):
        here = pl.ds(natural(x, parity), 1)
        sends[x, 85:88] = jnp.zeros((3, lat_cells), f32)
        sums = [None] * 5
        for m in range(members):
            weight = by_level([expo[m, k, here] for k in range(len(radii))], level_radius[...])
            for f in range(5):
                row = final_row(m, f, x, core, edge, rest)
                term = weight * row
                sums[f] = term if sums[f] is None else sums[f] + term
        for f in range(5):
            sends[x, 16 * f : 16 * f + 16] = sums[f]


def combine_kernel(level_radius, parts, result):
    sources = parts.shape[0]
    logs = [parts[d, 80:85] for d in range(sources)]
    best = logs[0]
    for d in range(1, sources):
        best = jnp.maximum(best, logs[d])
    scales = [jnp.exp(logs[d] - best) for d in range(sources)]
    total = scales[0]
    for d in range(1, sources):
        total = total + scales[d]
    over = 1.0 / total
    sums = [None] * 5
    for d in range(sources):
        share = scales[d] * over
        weight = by_level([share[k : k + 1] for k in range(len(radii))], level_radius[...])
        for f in range(5):
            term = weight * parts[d, 16 * f : 16 * f + 16]
            sums[f] = term if sums[f] is None else sums[f] + term
    for f in range(5):
        for d in range(sources):
            result[d, 16 * f : 16 * f + 16] = sums[f]


def blend_kernel(mean, core, edge, rest, out, done, sems):
    members = core.shape[0]
    parity = lax.rem(lax.axis_index("space"), 2)
    copies = []
    for m in range(members):
        for part in range(2):
            for k in range(4 * part, 4 * part + 4):
                for f in range(5):
                    row = final_row(m, f, k, core, edge, rest)
                    done[m, f, natural(k, parity)] = row + blend_share * (mean[k, 16 * f : 16 * f + 16] - row)
            rows = pl.ds(4 * (part + parity * (1 - 2 * part)), 4)
            copy = pltpu.make_async_copy(done.at[m, :, rows], out.at[m, :, rows], sems.at[m, part])
            copy.start()
            copies.append(copy)
    for copy in copies:
        copy.wait()


def local(state, diffusion, radius, obs_cells, obs_count, obs_value, obs_error):
    members, fields, width, levels, lat_cells = state.shape
    size = lax.axis_size("space")
    parity = (lax.axis_index("space") & 1).astype(jnp.int32).reshape(1)
    beside_pairs = [(i, i + 1 - 2 * (i % 2)) for i in range(size)]
    beyond_pairs = [(i, (i - 1 + 2 * (i % 2)) % size) for i in range(size)]

    orders = ((0, 2, 4, 6, 1, 3, 5, 7), (6, 4, 2, 0, 7, 5, 3, 1))
    groups = [[m * size + t for m in orders[t % 2]] for t in range(size)]

    def shape(*dims):
        return jax.ShapeDtypeStruct(dims, f32)

    near = lax.dynamic_slice_in_dim(state, 6 * (1 - parity[0]), 2, axis=2)
    far_a = lax.dynamic_slice_in_dim(state[:, :3], 6 * parity[0], 2, axis=2)
    near = lax.ppermute(near, "space", beside_pairs)
    far_a = lax.ppermute(far_a, "space", beyond_pairs)
    core, once_one, pre_zero, pre_one, column, grids, level_radius, far_b, rates = pl.pallas_call(
        interior_kernel,
        out_shape=(
            shape(members, fields, 6, levels, lat_cells),
            shape(members, fields, levels, lat_cells),
            shape(members, fields, levels, lat_cells),
            shape(members, fields, levels, lat_cells),
            shape(members, width, lat_cells),
            shape(3, width, lat_cells),
            jax.ShapeDtypeStruct((levels, lat_cells), jnp.int32),
            shape(members, 2, 2, levels, lat_cells),
            shape(8, lat_cells),
        ),
        in_specs=[vmem, vmem, smem, smem, vmem, smem, vmem, vmem],
        scratch_shapes=[pltpu.VMEM((fields, 8, levels, lat_cells), f32)],
        name="interior",
        compiler_params=room,
    )(state, near, diffusion, radius, obs_cells, obs_count, obs_value, obs_error)
    far_b = lax.ppermute(far_b, "space", beyond_pairs)
    edge, winds, grid = pl.pallas_call(
        far_kernel,
        out_shape=(
            shape(members, 3, 2, levels, lat_cells),
            shape(members, 2, levels, lat_cells),
            shape(members, width, lat_cells),
        ),
        in_specs=[vmem] * 8,
        scratch_shapes=[pltpu.VMEM((members, width, lat_cells), f32)],
        name="edges",
        compiler_params=room,
    )(state, rates, far_a, once_one, pre_zero, pre_one, column, grids)
    beside = lax.ppermute(grid, "space", beside_pairs)
    beyond = lax.ppermute(grid, "space", beyond_pairs)
    rest = pl.pallas_call(
        far_rest_kernel,
        out_shape=shape(members, 2, 2, levels, lat_cells),
        in_specs=[vmem] * 8,
        name="edges_rest",
        compiler_params=room,
    )(state, rates, far_a, far_b, once_one, pre_zero, pre_one, winds)
    sends = pl.pallas_call(
        weights_kernel,
        out_shape=shape(width, 88, lat_cells),
        in_specs=[vmem] * 7,
        scratch_shapes=[
            pltpu.VMEM((members, 24, lat_cells), f32),
            pltpu.VMEM((members, reach + 1, 2, 24, lat_cells // 2), f32),
            pltpu.VMEM((members, len(radii), width, lat_cells), f32),
        ],
        name="weights",
        compiler_params=room,
    )(level_radius, grid, beside, beyond, core, edge, rest)
    parts = lax.all_to_all(sends, ("mem", "space"), 0, 0, tiled=True, axis_index_groups=groups)
    share = pl.pallas_call(
        combine_kernel,
        out_shape=shape(width, 80, lat_cells),
        in_specs=[vmem] * 2,
        name="combine",
        compiler_params=room,
    )(level_radius, parts)
    mean = lax.all_to_all(share, ("mem", "space"), 0, 0, tiled=True, axis_index_groups=groups)
    return pl.pallas_call(
        blend_kernel,
        out_shape=shape(*state.shape),
        in_specs=[vmem] * 4,
        out_specs=anywhere,
        scratch_shapes=[pltpu.VMEM(state.shape, f32), pltpu.SemaphoreType.DMA((members, 2))],
        name="blend",
        compiler_params=room,
    )(mean, core, edge, rest)


def solution(mesh):
    return jax.shard_map(
        local,
        mesh=mesh,
        in_specs=(
            P("mem", None, "space", None, None),
            P(),
            P(),
            P("space", None),
            P("space"),
            P("space", None),
            P("space", None),
        ),
        out_specs=P("mem", None, "space", None, None),
        check_vma=False,
    )
```
